512 devices in a mesh: dp: 128 (over z, y, core), split: 4 (over x).
Axes of the slice: x: 4, y: 4, z: 16, core: 2. Of those that a mesh axis runs over, the one named last changes fastest.
Arguments:
- features: bfloat16 [262144, 1024], P(('dp', 'split')), may hold values from -60 to 60
- proj_weight: bfloat16 [1024, 768], replicated, may hold values from -0.1875 to 0.1875
- row_cluster: int32 [262144], P(('dp', 'split')), may hold values from -1 to 127, as said below
- row_rank: int32 [262144], P(('dp', 'split')), may hold values from -1 to 2047, as said below
- owner_slot: int32 [128], replicated, may hold values from 0 to 127, as said below
- tile_size: int32 [128], replicated, may hold values from 1024 to 2048
Outputs:
- max_sim: float32 [128, 2048], P('dp', 'split')
The draws below stay inside these ranges and needn't reach their ends.
Inputs may be any that keep to these rules, and one draw needn't show every extreme that they name: Cluster c is named by exactly tile_size[c] rows, whose row_rank values are 0 to tile_size[c] - 1, each once. Grouping named rows by owner_slot[row_cluster] // 1 and row_rank // 512, the 512 rows of one device put at most 1 row into one group, and some group gets exactly 1 from every device. `row_rank`: -1 exactly where row_cluster is -1. A permutation of 0 to 127; cluster c is held by dp index owner_slot[c].
All inputs are finite; a program needn't handle non-finite values.
Results may differ from the reference program's by a relative error of at most 0.0003.
Values may be sent and summed in bfloat16 or wider, within the bound.
No kernel may reach another device: no remote copies, remote signals or barrier semaphores. Data moves between devices by JAX's collectives and lax.ppermute only.
A program may use at most 64 MiB of HBM per device.

```python
import jax
import jax.numpy as jnp
from jax import lax

FEAT = 1024
EMB = 768
TILE = 2048
CL_DEV = 1
CLUSTERS = 128
BLK = 512
ROWS_DEV = 512
ROWS = 262144
CAP = 1
DEVICES = 512


def window_plan(key):
    key_owner, key_size, key_sender, key_local = jax.random.split(key, 4)
    owner_slot = jax.random.permutation(key_owner, CLUSTERS).astype(jnp.int32)
    sizes = jax.random.randint(key_size, (CLUSTERS,), TILE // 2, TILE + 1).astype(jnp.int32)
    sizes = sizes.at[0].set(TILE).at[1].set(TILE // 2)
    cluster_at = jnp.argsort(owner_slot).astype(jnp.int32)
    senders = jax.vmap(lambda sub_key: jax.random.permutation(sub_key, DEVICES))(jax.random.split(key_sender, DEVICES))
    first_slot = jnp.argsort(senders, axis=1).astype(jnp.int32)
    copies = jnp.arange(CAP, dtype=jnp.int32) * DEVICES
    position = first_slot.T[:, :, None] + copies[None, None, :]
    receiver = jnp.arange(DEVICES, dtype=jnp.int32)[None, :, None]
    splits = TILE // BLK
    owner_index = receiver // splits
    block_index = receiver % splits
    held_slot = owner_index * CL_DEV + position // BLK
    member_rank = block_index * BLK + position % BLK
    cluster = cluster_at[held_slot]
    living = member_rank < sizes[cluster]
    cluster_rows = jnp.where(living, cluster, -1).reshape(DEVICES, ROWS_DEV)
    rank_rows = jnp.where(living, member_rank, -1).reshape(DEVICES, ROWS_DEV)
    shuffle = jax.vmap(lambda sub_key: jax.random.permutation(sub_key, ROWS_DEV))(jax.random.split(key_local, DEVICES))
    inverse = jnp.argsort(shuffle, axis=1)
    cluster_rows = jnp.take_along_axis(cluster_rows, inverse, axis=1).reshape(ROWS).astype(jnp.int32)
    rank_rows = jnp.take_along_axis(rank_rows, inverse, axis=1).reshape(ROWS).astype(jnp.int32)
    return (owner_slot, sizes, cluster_rows, rank_rows)


def draw_owner_slot(key, part):
    return window_plan(key)[0]


def draw_tile_size(key, part):
    return window_plan(key)[1]


def draw_row_cluster(key, part):
    return window_plan(key)[2]


def draw_row_rank(key, part):
    return window_plan(key)[3]


def draw_features(key, part):
    cluster_rows = window_plan(key)[2]
    key = jax.random.fold_in(key, 7)
    key_centre, key_strength, key_noise = jax.random.split(key, 3)
    centres = jax.random.truncated_normal(key_centre, -4.0, 4.0, (CLUSTERS, FEAT), jnp.float32)
    strength = jax.random.uniform(key_strength, (ROWS, 1), jnp.float32, 0.3, 1.5)
    noise = jax.random.truncated_normal(key_noise, -4.0, 4.0, (ROWS, FEAT), jnp.float32)
    member = (cluster_rows >= 0).astype(jnp.float32)[:, None]
    values = strength * member * centres[jnp.maximum(cluster_rows, 0)] + noise
    return values.astype(jnp.bfloat16)


def gaussian(stream_key, dims, spread, reach, kind=jnp.bfloat16):
    result = spread * jax.random.normal(stream_key, dims, jnp.float32)
    return jnp.clip(result, min=-reach, max=reach).astype(kind)


def setup_inputs(seed: int = 0) -> dict:
    streams_of = jax.random.split(jax.random.key(seed), 7)
    features = draw_features(jax.random.fold_in(streams_of[6], 71), 0)
    proj_weight = gaussian(streams_of[1], (FEAT, EMB), FEAT ** -0.5, 0.1875)
    row_cluster = draw_row_cluster(jax.random.fold_in(streams_of[6], 71), 0)
    row_rank = draw_row_rank(jax.random.fold_in(streams_of[6], 71), 0)
    owner_slot = draw_owner_slot(jax.random.fold_in(streams_of[6], 71), 0)
    tile_size = draw_tile_size(jax.random.fold_in(streams_of[6], 71), 0)
    return {"features": features, "proj_weight": proj_weight, "row_cluster": row_cluster, "row_rank": row_rank, "owner_slot": owner_slot, "tile_size": tile_size}


def reference(features, proj_weight, row_cluster, row_rank, owner_slot, tile_size):
    live = row_cluster >= 0
    slot_of_row = owner_slot[jnp.maximum(row_cluster, 0)]
    flat_index = jnp.where(live, slot_of_row * TILE + row_rank, CLUSTERS * TILE).astype(jnp.int32)
    tile_rows = jnp.full((CLUSTERS * TILE,), ROWS, jnp.int32)
    tile_rows = tile_rows.at[flat_index].set(jnp.arange(ROWS, dtype=jnp.int32), mode='drop')
    tile_rows = tile_rows.reshape(CLUSTERS, TILE)
    slot_size = jnp.zeros((CLUSTERS,), jnp.int32).at[owner_slot].set(tile_size)
    ranks = jnp.arange(TILE, dtype=jnp.int32)

    def one_tile(packed):
        indices, size_here = packed
        gathered = jnp.take(features, indices, axis=0, mode='fill', fill_value=0)
        projected = jnp.dot(gathered, proj_weight, preferred_element_type=jnp.float32)
        normed = projected * lax.rsqrt(lax.optimization_barrier(jnp.sum(projected * projected, axis=1, keepdims=True)) + 1e-06)
        normed = normed.astype(jnp.bfloat16)
        scores = jnp.dot(normed, normed.T, preferred_element_type=jnp.float32)
        earlier = ranks[None, :] < ranks[:, None]
        best = lax.optimization_barrier(jnp.max(jnp.where(earlier, scores, -1.0), axis=1))
        return jnp.where(ranks < size_here, best, -1.0).astype(jnp.float32)
    return lax.map(one_tile, (tile_rows, slot_size))
```

```python
import jax
import jax.numpy as jnp
from jax import lax
from jax.experimental import pallas as pl
from jax.experimental.pallas import tpu as pltpu
from jax.sharding import PartitionSpec as P

TILE = 2048
EPS = 1e-06
AXES = ("dp", "split")
NT = (((1,), (1,)), ((), ()))
TN = (((0,), (0,)), ((), ()))


def iota(shape, dim):
    return lax.broadcasted_iota(jnp.int32, shape, dim)


def bf16(mask_or_int):
    return mask_or_int.astype(jnp.float32).astype(jnp.bfloat16)


def project_kernel(splits, block, features_ref, weight_ref, cluster_ref, rank_ref, owner_ref, out_ref):
    cluster, rank = cluster_ref[...], rank_ref[...]
    clusters, rows, width = owner_ref.shape[1], cluster.shape[1], weight_ref.shape[1]
    projected = jnp.dot(features_ref[...], weight_ref[...], preferred_element_type=jnp.float32)
    normed = projected * lax.rsqrt(jnp.sum(projected * projected, axis=1, keepdims=True) + EPS)
    normed = normed.astype(jnp.bfloat16)

    owner = bf16(jnp.broadcast_to(owner_ref[...], (8, clusters)))
    named = bf16(iota((clusters, rows), 0) == cluster)
    slot = jnp.dot(owner, named, preferred_element_type=jnp.float32)[0:1].astype(jnp.int32)
    place = jnp.where(cluster >= 0, slot * splits + rank // block, -1)
    high, low = (rank + 1) // 16, (rank + 1) % 16
    lane = iota((128, rows), 0)
    numbers = jnp.zeros((rows // 2, 128), jnp.float32)
    for i in range(2):
        chosen = bf16(2 * iota((rows // 2, rows), 0) + i == place)
        sent = jnp.dot(chosen, normed, preferred_element_type=jnp.float32)
        out_ref[:, i * width : (i + 1) * width] = sent.astype(jnp.bfloat16)
        digits = bf16(jnp.where(lane == 2 * i, high, jnp.where(lane == 2 * i + 1, low, 0)))
        numbers += lax.dot_general(chosen, digits, NT, preferred_element_type=jnp.float32)
    out_ref[:, 2 * width :] = numbers.astype(jnp.bfloat16)


def gram_kernel(width, index_ref, owner_ref, size_ref, *refs):
    out_ref = refs[-1]
    block = out_ref.shape[1]
    start = index_ref[1] * block
    rank = start + iota((1, block), 1)
    number = (rank + 1).astype(jnp.float32)
    parts = []
    mine = jnp.zeros((block, width), jnp.float32)
    for ref in refs[:-1]:
        rows = jnp.concatenate([ref[:, :width], ref[:, width : 2 * width]], axis=0)
        digits = ref[:, 2 * width :].astype(jnp.float32)
        label = jnp.concatenate([digits[:, i : i + 1] * 16 + digits[:, i + 1 : i + 2] for i in (0, 2)], axis=0)
        chosen = bf16(label == number)
        mine += lax.dot_general(chosen, rows, TN, preferred_element_type=jnp.float32)
        parts.append((rows, label))
    mine = mine.astype(jnp.bfloat16)
    best = jnp.full((8, block), -1.0, jnp.float32)
    for rows, label in parts:
        scores = lax.dot_general(rows, mine, NT, preferred_element_type=jnp.float32)
        scores = jnp.where((label > 0) & (label < number), scores, -1.0)
        best = jnp.maximum(best, jnp.max(scores.reshape(-1, 8, block), axis=0))
    best = jnp.max(best, axis=0, keepdims=True)
    size = jnp.sum(jnp.where(owner_ref[...] == index_ref[0], size_ref[...], 0), axis=1, keepdims=True)
    out_ref[...] = jnp.where(rank < size, best, -1.0)


def local(features, proj_weight, row_cluster, row_rank, owner_slot, tile_size):
    owners, splits = lax.axis_size("dp"), lax.axis_size("split")
    planes = owners // (2 * splits)
    rows, width = features.shape[0], proj_weight.shape[1]
    block = TILE // splits
    vmem = pl.BlockSpec(memory_space=pltpu.VMEM)
    smem = pl.BlockSpec(memory_space=pltpu.SMEM)
    params = pltpu.CompilerParams(vmem_limit_bytes=40 * 1024 * 1024)
    owner_row = owner_slot.reshape(1, -1)

    def device(z, y, core, x):
        return ((z * splits + y) * 2 + core) * splits + x

    everywhere = [(z, a, b) for z in range(planes) for a in range(splits) for b in range(splits)]
    diagonals = [
        [
            device(z, (g - j) % splits, 1, j) if core else device(z, j, 0, (g - j) % splits)
            for z in range(planes)
            for j in range(splits)
            for core in range(2)
        ]
        for g in range(splits)
    ]

    def shift(array, step):
        pairs = [(device(z, a, 0, b), device(z, a, 0, (b + step) % splits)) for z, a, b in everywhere]
        pairs += [(device(z, a, 1, b), device(z, (a + step) % splits, 1, b)) for z, a, b in everywhere]
        return lax.ppermute(array, AXES, pairs)

    outgoing = pl.pallas_call(
        lambda *refs: project_kernel(splits, block, *refs),
        out_shape=jax.ShapeDtypeStruct((rows // 2, 2 * width + 128), jnp.bfloat16),
        in_specs=[vmem] * 5,
        out_specs=vmem,
        compiler_params=params,
        name="project",
    )(features, proj_weight, row_cluster.reshape(1, rows), row_rank.reshape(1, rows), owner_row)

    own = lax.all_to_all(
        outgoing.reshape(owners, splits // 2, -1), AXES, 0, 0, tiled=True, axis_index_groups=diagonals
    ).reshape(rows // 2, -1)
    first, second = own[: rows // 4], own[rows // 4 :]
    left_first, right_second = shift(first, 1), shift(second, -1)
    left_second, right_first = shift(second, 1), shift(first, -1)
    far_first, far_second = shift(left_first, 1), shift(right_second, -1)

    owner, x = lax.axis_index("dp"), lax.axis_index("split")
    z, y, core = owner // (2 * splits), owner // 2 % splits, owner % 2
    index = jnp.stack(
        [jnp.where(core == 0, owner, (z * splits + x) * 2 + 1), jnp.where(core == 0, x, y)]
    ).astype(jnp.int32)
    best = pl.pallas_call(
        lambda *refs: gram_kernel(width, *refs),
        out_shape=jax.ShapeDtypeStruct((1, block), jnp.float32),
        in_specs=[smem] + [vmem] * 9,
        out_specs=vmem,
        compiler_params=params,
        name="gram",
    )(index, owner_row, tile_size.reshape(1, -1), own, left_first, right_second, left_second, right_first, far_first, far_second)
    home = [(device(z, a, 0, b), device(z, a, 0, b)) for z, a, b in everywhere]
    home += [(device(z, a, 1, b), device(z, b, 1, a)) for z, a, b in everywhere]
    return lax.ppermute(best, AXES, home)


def solution(mesh):
    return jax.shard_map(
        local,
        mesh=mesh,
        in_specs=(P(("dp", "split"), None), P(), P(("dp", "split")), P(("dp", "split")), P(), P()),
        out_specs=P("dp", "split"),
        check_vma=False,
    )
```

```python
import jax
import jax.numpy as jnp
from jax import lax
from jax.experimental import pallas as pl
from jax.experimental.pallas import tpu as pltpu
from jax.sharding import PartitionSpec as P

TILE = 2048
EPS = 1e-06
AXES = ("dp", "split")
NT = (((1,), (1,)), ((), ()))
FAR = 1e9


def iota(shape, dim):
    return lax.broadcasted_iota(jnp.int32, shape, dim)


def bf16(mask_or_int):
    return mask_or_int.astype(jnp.float32).astype(jnp.bfloat16)


def project_kernel(
    splits, block, features_hbm, weight_hbm, cluster_hbm, rank_hbm, owner_hbm, out_ref,
    features, weight, cluster_ref, rank_ref, owner_ref, semaphores,
):
    half = features.shape[1] // 2
    copies = []
    for i in range(2):
        part = pl.ds(i * half, half)
        copies.append((weight_hbm.at[part, :], weight.at[part, :]))
        copies.append((features_hbm.at[:, part], features.at[:, part]))
    copies += [(cluster_hbm, cluster_ref), (rank_hbm, rank_ref), (owner_hbm, owner_ref)]
    copies = [pltpu.make_async_copy(*pair, semaphores.at[i]) for i, pair in enumerate(copies)]
    for copy in copies[4:] + copies[:4]:
        copy.start()
    for copy in copies[4:]:
        copy.wait()
    cluster, rank = cluster_ref[...], rank_ref[...]
    clusters, rows, width = owner_ref.shape[1], cluster.shape[1], weight.shape[1]
    owner = bf16(jnp.broadcast_to(owner_ref[...], (8, clusters)))
    named = bf16(iota((clusters, rows), 0) == cluster)
    slot = jnp.dot(owner, named, preferred_element_type=jnp.float32)[0:1].astype(jnp.int32)
    place = jnp.where(cluster >= 0, slot * splits + rank // block, -1)
    high, low = (rank + 1) // 16, (rank + 1) % 16
    lane = iota((128, rows), 0)
    numbers = jnp.zeros((rows // 2, 128), jnp.float32)
    chosen = [bf16(2 * iota((rows // 2, rows), 0) + i == place) for i in range(2)]
    for i in range(2):
        digits = bf16(jnp.where(lane == 2 * i, high, jnp.where(lane == 2 * i + 1, low, 0)))
        numbers += lax.dot_general(chosen[i], digits, NT, preferred_element_type=jnp.float32)
    out_ref[:, 2 * width :] = numbers.astype(jnp.bfloat16)

    copies[0].wait()
    copies[1].wait()
    projected = jnp.dot(features[:, :half], weight[:half, :], preferred_element_type=jnp.float32)
    copies[2].wait()
    copies[3].wait()
    projected += jnp.dot(features[:, half:], weight[half:, :], preferred_element_type=jnp.float32)
    normed = projected * lax.rsqrt(jnp.sum(projected * projected, axis=1, keepdims=True) + EPS)
    normed = normed.astype(jnp.bfloat16)
    for i in range(2):
        sent = jnp.dot(chosen[i], normed, preferred_element_type=jnp.float32)
        out_ref[:, i * width : (i + 1) * width] = sent.astype(jnp.bfloat16)


class Members:
    def __init__(self, ref, width, step):
        self.ref, self.width, self.step = ref, width, step

    def number(self, digits, first):
        weight = jnp.where(iota((128, self.step), 0) == first, 16, jnp.where(iota((128, self.step), 0) == first + 1, 1, 0))
        return jnp.dot(digits, bf16(weight), preferred_element_type=jnp.float32)

    def halves(self):
        digits = self.ref[:, 2 * self.width :]
        for i in range(2):
            number = self.number(digits, 2 * i)
            yield self.ref[:, i * self.width : (i + 1) * self.width], jnp.where(number > 0, number, FAR)

    def own(self, block_index):
        start = pl.multiple_of(block_index // 2 * self.step, self.step)
        column = pl.multiple_of(block_index % 2 * self.width, 128)
        rows = self.ref[pl.ds(start, self.step), pl.ds(column, self.width)]
        digits = self.ref[pl.ds(start, self.step), 2 * self.width :]
        first = 2 * (block_index % 2)
        weight = jnp.where(iota((8, 128), 1) == first, 16, jnp.where(iota((8, 128), 1) == first + 1, 1, 0))
        along = lax.dot_general(bf16(weight), digits, NT, preferred_element_type=jnp.float32)[0:1]
        return rows, along, self.number(digits, first)


def earlier_max(best, members, queries, numbers):
    step = numbers[0].shape[1]
    for part in members:
        for rows, number in part.halves():
            scores = lax.dot_general(rows, queries, NT, preferred_element_type=jnp.float32)
            for i, query_number in enumerate(numbers):
                found = jnp.where(number < query_number, scores[:, i * step : (i + 1) * step], -1.0)
                best[i] = jnp.maximum(best[i], jnp.max(found.reshape(-1, 8, step), axis=0))
    return best


def near_kernel(width, step, index_ref, own_ref, left_ref, right_ref, out_ref):
    parts = [Members(ref, width, step) for ref in (own_ref, left_ref, right_ref)]
    rows, numbers, _ = zip(*[part.own(index_ref[1]) for part in parts])
    best = [jnp.full((8, step), -1.0, jnp.float32) for _ in parts]
    best = earlier_max(best, parts, jnp.concatenate(rows, axis=0), numbers)
    for i, found in enumerate(best):
        out_ref[:, i * step : (i + 1) * step] = found


def far_kernel(width, step, index_ref, owner_ref, size_ref, own_ref, left_ref, right_ref, far_ref, near_ref, out_ref):
    block = out_ref.shape[1]
    parts = [Members(ref, width, step) for ref in (own_ref, left_ref, right_ref, far_ref)]
    rows, numbers, columns = zip(*[part.own(index_ref[1]) for part in parts])
    best = [near_ref[:, i * step : (i + 1) * step] for i in range(3)] + [jnp.full((8, step), -1.0, jnp.float32)]
    best[3:] = earlier_max(best[3:], parts[:3], rows[3], numbers[3:])
    best = earlier_max(best, parts[3:], jnp.concatenate(rows, axis=0), numbers)
    best = jnp.concatenate([jnp.max(found, axis=0, keepdims=True) for found in best], axis=1)

    start = index_ref[1] * block
    target = (start + 1 + iota((1, block), 1)).astype(jnp.float32)
    chosen = jnp.concatenate(
        [
            jnp.concatenate([bf16(column == target[:, i * step : (i + 1) * step]) for i in range(block // step)], axis=1)
            for column in columns
        ],
        axis=0,
    )
    first = best.astype(jnp.bfloat16)
    rest = best - first.astype(jnp.float32)
    second = rest.astype(jnp.bfloat16)
    third = (rest - second.astype(jnp.float32)).astype(jnp.bfloat16)
    line = iota((8, best.shape[1]), 0)
    terms = [jnp.broadcast_to(term.astype(jnp.float32), line.shape) for term in (first, second, third)]
    split = jnp.where(line == 0, terms[0], jnp.where(line == 1, terms[1], jnp.where(line == 2, terms[2], 0.0)))
    found = jnp.dot(split.astype(jnp.bfloat16), chosen, preferred_element_type=jnp.float32)
    ordered = found[0:1] + found[1:2] + found[2:3]
    size = jnp.sum(jnp.where(owner_ref[...] == index_ref[0], size_ref[...], 0), axis=1, keepdims=True)
    out_ref[...] = jnp.where(start + iota((1, block), 1) < size, ordered, -1.0)


def local(features, proj_weight, row_cluster, row_rank, owner_slot, tile_size):
    owners, splits = lax.axis_size("dp"), lax.axis_size("split")
    planes = owners // (2 * splits)
    rows, width = features.shape[0], proj_weight.shape[1]
    block = TILE // splits
    hbm = pl.BlockSpec(memory_space=pl.ANY)
    vmem = pl.BlockSpec(memory_space=pltpu.VMEM)
    smem = pl.BlockSpec(memory_space=pltpu.SMEM)
    params = pltpu.CompilerParams(vmem_limit_bytes=40 * 1024 * 1024)
    owner_row = owner_slot.reshape(1, -1)

    def device(z, y, core, x):
        return ((z * splits + y) * 2 + core) * splits + x

    everywhere = [(z, a, b) for z in range(planes) for a in range(splits) for b in range(splits)]
    diagonals = [
        [
            device(z, (g - j) % splits, 1, j) if core else device(z, j, 0, (g - j) % splits)
            for z in range(planes)
            for j in range(splits)
            for core in range(2)
        ]
        for g in range(splits)
    ]

    def shift(array, step):
        pairs = [(device(z, a, 0, b), device(z, a, 0, (b + step) % splits)) for z, a, b in everywhere]
        pairs += [(device(z, a, 1, b), device(z, (a + step) % splits, 1, b)) for z, a, b in everywhere]
        return lax.ppermute(array, AXES, pairs)

    outgoing = pl.pallas_call(
        lambda *refs: project_kernel(splits, block, *refs),
        out_shape=jax.ShapeDtypeStruct((rows // 2, 2 * width + 128), jnp.bfloat16),
        in_specs=[hbm] * 5,
        out_specs=vmem,
        scratch_shapes=[
            pltpu.VMEM(features.shape, jnp.bfloat16),
            pltpu.VMEM(proj_weight.shape, jnp.bfloat16),
            pltpu.VMEM((1, rows), jnp.int32),
            pltpu.VMEM((1, rows), jnp.int32),
            pltpu.VMEM(owner_row.shape, jnp.int32),
            pltpu.SemaphoreType.DMA((7,)),
        ],
        compiler_params=pltpu.CompilerParams(vmem_limit_bytes=60 * 1024 * 1024),
        name="project",
    )(features, proj_weight, row_cluster.reshape(1, rows), row_rank.reshape(1, rows), owner_row)

    own = lax.all_to_all(
        outgoing.reshape(owners, splits // 2, -1), AXES, 0, 0, tiled=True, axis_index_groups=diagonals
    )
    own = own.transpose(1, 0, 2).reshape(rows // 2, -1)
    left, right, far = shift(own, 1), shift(own, -1), shift(own, 2)

    owner, x = lax.axis_index("dp"), lax.axis_index("split")
    z, y, core = owner // (2 * splits), owner // 2 % splits, owner % 2
    index = jnp.stack(
        [jnp.where(core == 0, owner, (z * splits + x) * 2 + 1), jnp.where(core == 0, x, y)]
    ).astype(jnp.int32)
    near_best = pl.pallas_call(
        lambda *refs: near_kernel(width, owners, *refs),
        out_shape=jax.ShapeDtypeStruct((8, 3 * owners), jnp.float32),
        in_specs=[smem] + [vmem] * 3,
        out_specs=vmem,
        compiler_params=params,
        name="near",
        cost_estimate=pl.CostEstimate(flops=2 * 3 * owners * 3 * rows * width, bytes_accessed=3 << 20, transcendentals=0),
    )(index, own, left, right)
    best = pl.pallas_call(
        lambda *refs: far_kernel(width, owners, *refs),
        out_shape=jax.ShapeDtypeStruct((1, block), jnp.float32),
        in_specs=[smem] + [vmem] * 7,
        out_specs=vmem,
        compiler_params=params,
        name="far",
    )(index, owner_row, tile_size.reshape(1, -1), own, left, right, far, near_best)
    home = [(device(z, a, 0, b), device(z, a, 0, b)) for z, a, b in everywhere]
    home += [(device(z, a, 1, b), device(z, b, 1, a)) for z, a, b in everywhere]
    return lax.ppermute(best, AXES, home)


def solution(mesh):
    return jax.shard_map(
        local,
        mesh=mesh,
        in_specs=(P(("dp", "split"), None), P(), P(("dp", "split")), P(("dp", "split")), P(), P()),
        out_specs=P("dp", "split"),
        check_vma=False,
    )
```

```python
import jax
import jax.numpy as jnp
from jax import lax
from jax.experimental import pallas as pl
from jax.experimental.pallas import tpu as pltpu
from jax.sharding import PartitionSpec as P

TILE = 2048
EPS = 1e-06
NT = (((1,), (1,)), ((), ()))
FAR = 1e9


def iota(shape, dim):
    return lax.broadcasted_iota(jnp.int32, shape, dim)


def bf16(mask_or_int):
    return mask_or_int.astype(jnp.float32).astype(jnp.bfloat16)


def project_kernel(
    splits, block, features_hbm, weight_hbm, member_ref, owner_ref, out_ref, features, weight, semaphores,
):
    steps = 4
    part = features.shape[1] // steps
    pairs = []
    for i in range(steps):
        span = pl.ds(i * part, part)
        pairs.append((weight_hbm.at[span, :], weight.at[span, :]))
        pairs.append((features_hbm.at[:, span], features.at[:, span]))
    copies = [pltpu.make_async_copy(*pair, semaphores.at[i]) for i, pair in enumerate(pairs)]
    for copy in copies:
        copy.start()
    member = member_ref[...]
    clusters, rows, width = owner_ref.shape[1], member.shape[1], weight.shape[1]
    cluster, rank = member // TILE, member % TILE
    owner = bf16(jnp.broadcast_to(owner_ref[...], (8, clusters)))
    named = bf16(iota((clusters, rows), 0) == cluster)
    slot = jnp.dot(owner, named, preferred_element_type=jnp.float32)[0:1].astype(jnp.int32)
    place = jnp.where(member >= 0, slot * splits + rank // block, -1)
    high, low = (rank + 1) // 16, (rank + 1) % 16
    lane = iota((128, rows), 0)
    numbers = jnp.zeros((rows // 2, 128), jnp.float32)
    chosen = [bf16(2 * iota((rows // 2, rows), 0) + i == place) for i in range(2)]
    for i in range(2):
        digits = bf16(jnp.where(lane == 2 * i, high, jnp.where(lane == 2 * i + 1, low, 0)))
        numbers += lax.dot_general(chosen[i], digits, NT, preferred_element_type=jnp.float32)
    out_ref[:, 2 * width :] = numbers.astype(jnp.bfloat16)

    projected = jnp.zeros((rows, width), jnp.float32)
    for i in range(0, steps, 2):
        for copy in copies[2 * i : 4 + 2 * i]:
            copy.wait()
        span = slice(i * part, (i + 2) * part)
        projected += jnp.dot(features[:, span], weight[span, :], preferred_element_type=jnp.float32)
    normed = projected * lax.rsqrt(jnp.sum(projected * projected, axis=1, keepdims=True) + EPS)
    normed = normed.astype(jnp.bfloat16)
    for i in range(2):
        sent = jnp.dot(chosen[i], normed, preferred_element_type=jnp.float32)
        out_ref[:, i * width : (i + 1) * width] = sent.astype(jnp.bfloat16)


class Members:
    def __init__(self, ref, width, step):
        self.ref, self.width, self.step = ref, width, step

    def rows(self, index):
        span = slice(index // 2 * self.step, (index // 2 + 1) * self.step)
        return self.ref[span, index % 2 * self.width : (index % 2 + 1) * self.width]

    def weights(self, index, shape, dim):
        first = 2 * (index % 2)
        return bf16(jnp.where(iota(shape, dim) == first, 16, jnp.where(iota(shape, dim) == first + 1, 1, 0)))

    def digits(self, index):
        return self.ref[index // 2 * self.step : (index // 2 + 1) * self.step, 2 * self.width :]

    def down(self, index):
        weights = self.weights(index, (128, self.step), 0)
        return jnp.dot(self.digits(index), weights, preferred_element_type=jnp.float32)

    def along(self, index):
        weights = self.weights(index, (8, 128), 1)
        return lax.dot_general(weights, self.digits(index), NT, preferred_element_type=jnp.float32)[0:1]


def earlier_max(best, members, queries, numbers):
    splits, step = len(best), numbers[0].shape[1]
    for b in range(splits):
        rows = jnp.concatenate([part.rows(b) for part in members], axis=0)
        number = jnp.concatenate([part.down(b) for part in members], axis=0)
        number = jnp.where(number > 0, number, FAR)
        later = jnp.concatenate([queries.rows(a) for a in range(b, splits)], axis=0)
        scores = lax.dot_general(rows, later, NT, preferred_element_type=jnp.float32)
        for a in range(b, splits):
            found = jnp.where(number < numbers[a], scores[:, (a - b) * step : (a - b + 1) * step], -1.0)
            best[a] = jnp.maximum(best[a], jnp.max(found.reshape(-1, 8, step), axis=0))
    return best


def own_kernel(splits, width, step, own_ref, out_ref):
    own = Members(own_ref, width, step)
    best = [jnp.full((8, step), -1.0, jnp.float32) for _ in range(splits)]
    best = earlier_max(best, [own], own, [own.along(a) for a in range(splits)])
    for a in range(splits):
        out_ref[:, a * step : (a + 1) * step] = best[a]


def ring_kernel(splits, width, step, owner_index_ref, owner_ref, size_ref, own_ref, left_ref, right_ref, best_ref, out_ref):
    block = out_ref.shape[2]
    own, left, right = [Members(ref, width, step) for ref in (own_ref, left_ref, right_ref)]
    own_best = [best_ref[:, a * step : (a + 1) * step] for a in range(splits)]
    own_best = earlier_max(own_best, [left, right], own, [own.along(a) for a in range(splits)])
    left_best = [jnp.full((8, step), -1.0, jnp.float32) for _ in range(splits)]
    left_best = earlier_max(left_best, [right], left, [left.along(a) for a in range(splits)])

    size = jnp.sum(jnp.where(owner_ref[...] == owner_index_ref[0], size_ref[...], 0), axis=1, keepdims=True)
    for a in range(splits):
        rank = a * block + iota((1, block), 1)
        target = (rank + 1).astype(jnp.float32)
        column = jnp.concatenate([own.down(a), left.down(a)], axis=0)
        chosen = jnp.concatenate(
            [bf16(column == target[:, i * step : (i + 1) * step]) for i in range(block // step)], axis=1
        )
        best = jnp.concatenate(
            [jnp.max(own_best[a], axis=0, keepdims=True), jnp.max(left_best[a], axis=0, keepdims=True)], axis=1
        )
        first = best.astype(jnp.bfloat16)
        rest = best - first.astype(jnp.float32)
        second = rest.astype(jnp.bfloat16)
        third = (rest - second.astype(jnp.float32)).astype(jnp.bfloat16)
        line = iota((8, best.shape[1]), 0)
        terms = jnp.ones(line.shape, jnp.float32)
        for i, term in enumerate((first, second, third)):
            terms = jnp.where(line == i, term.astype(jnp.float32), terms)
        found = jnp.dot(terms.astype(jnp.bfloat16), chosen, preferred_element_type=jnp.float32)
        ordered = found[0:1] + found[1:2] + found[2:3]
        out_ref[a] = jnp.where((found[3:4] > 0) & (rank < size), ordered, -1.0)


def local(features, proj_weight, row_cluster, row_rank, owner_slot, tile_size):
    owners, splits = lax.axis_size("dp"), lax.axis_size("split")
    rows, width = features.shape[0], proj_weight.shape[1]
    block = TILE // splits
    hbm = pl.BlockSpec(memory_space=pltpu.HBM)
    vmem = pl.BlockSpec(memory_space=pltpu.VMEM)
    smem = pl.BlockSpec(memory_space=pltpu.SMEM)
    params = pltpu.CompilerParams(vmem_limit_bytes=32 * 1024 * 1024)
    owner_row = owner_slot.reshape(1, -1)
    member = jnp.where(row_cluster >= 0, row_cluster * TILE + row_rank, -1)

    outgoing = pl.pallas_call(
        lambda *refs: project_kernel(splits, block, *refs),
        out_shape=jax.ShapeDtypeStruct((rows // 2, 2 * width + 128), jnp.bfloat16),
        in_specs=[hbm] * 2 + [vmem] * 2,
        out_specs=vmem,
        scratch_shapes=[
            pltpu.VMEM(features.shape, jnp.bfloat16),
            pltpu.VMEM(proj_weight.shape, jnp.bfloat16),
            pltpu.SemaphoreType.DMA((8,)),
        ],
        compiler_params=pltpu.CompilerParams(vmem_limit_bytes=55200000),
        name="project",
    )(features, proj_weight, member.reshape(1, rows), owner_row)

    own = lax.all_to_all(outgoing.reshape(owners, splits // 2, -1), "dp", 0, 0, tiled=True)
    own = own.transpose(1, 0, 2).reshape(rows // 2, -1)
    left = lax.ppermute(own, "split", [(i, (i + 1) % splits) for i in range(splits)])
    right = lax.ppermute(own, "split", [(i, (i - 1) % splits) for i in range(splits)])

    best = pl.pallas_call(
        lambda *refs: own_kernel(splits, width, owners, *refs),
        out_shape=jax.ShapeDtypeStruct((8, splits * owners), jnp.float32),
        in_specs=[vmem],
        out_specs=vmem,
        compiler_params=params,
        name="own",
        cost_estimate=pl.CostEstimate(flops=2 * rows * rows * width, bytes_accessed=2 << 20, transcendentals=0),
    )(own)
    best = pl.pallas_call(
        lambda *refs: ring_kernel(splits, width, owners, *refs),
        out_shape=jax.ShapeDtypeStruct((splits, 1, block), jnp.float32),
        in_specs=[smem] + [vmem] * 6,
        out_specs=vmem,
        compiler_params=params,
        name="ring",
    )(lax.axis_index("dp").reshape(1), owner_row, tile_size.reshape(1, -1), own, left, right, best)
    return jnp.max(lax.all_to_all(best, "split", 0, 0, tiled=True), axis=0)


def solution(mesh):
    return jax.shard_map(
        local,
        mesh=mesh,
        in_specs=(P(("dp", "split"), None), P(), P(("dp", "split")), P(("dp", "split")), P(), P()),
        out_specs=P("dp", "split"),
        check_vma=False,
    )
```

```python
import jax
import jax.numpy as jnp
from jax import lax
from jax.experimental import pallas as pl
from jax.experimental.pallas import tpu as pltpu
from jax.sharding import PartitionSpec as P

TILE = 2048
EPS = 1e-06
AXES = ("dp", "split")
NT = (((1,), (1,)), ((), ()))
FAR = 1e9


def iota(shape, dim):
    return lax.broadcasted_iota(jnp.int32, shape, dim)


def bf16(mask_or_int):
    return mask_or_int.astype(jnp.float32).astype(jnp.bfloat16)


def project_kernel(
    splits, block, features_hbm, weight_hbm, member_ref, owner_ref, out_ref, features, weight, semaphores,
):
    steps = 4
    part = features.shape[1] // steps
    pairs = []
    for i in range(steps):
        span = pl.ds(i * part, part)
        pairs.append((weight_hbm.at[span, :], weight.at[span, :]))
        pairs.append((features_hbm.at[:, span], features.at[:, span]))
    copies = [pltpu.make_async_copy(*pair, semaphores.at[i]) for i, pair in enumerate(pairs)]
    for copy in copies:
        copy.start()
    member = member_ref[...]
    clusters, rows, width = owner_ref.shape[1], member.shape[1], weight.shape[1]
    cluster, rank = member // TILE, member % TILE
    owner = bf16(jnp.broadcast_to(owner_ref[...], (8, clusters)))
    named = bf16(iota((clusters, rows), 0) == cluster)
    slot = jnp.dot(owner, named, preferred_element_type=jnp.float32)[0:1].astype(jnp.int32)
    place = jnp.where(member >= 0, slot * splits + rank // block, -1)
    high, low = (rank + 1) // 16, (rank + 1) % 16
    lane = iota((128, rows), 0)
    numbers = jnp.zeros((rows // 2, 128), jnp.float32)
    chosen = [bf16(2 * iota((rows // 2, rows), 0) + i == place) for i in range(2)]
    for i in range(2):
        digits = bf16(jnp.where(lane == 2 * i, high, jnp.where(lane == 2 * i + 1, low, 0)))
        numbers += lax.dot_general(chosen[i], digits, NT, preferred_element_type=jnp.float32)
    out_ref[:, 2 * width :] = numbers.astype(jnp.bfloat16)

    projected = jnp.zeros((rows, width), jnp.float32)
    for i in range(0, steps, 2):
        for copy in copies[2 * i : 4 + 2 * i]:
            copy.wait()
        span = slice(i * part, (i + 2) * part)
        projected += jnp.dot(features[:, span], weight[span, :], preferred_element_type=jnp.float32)
    normed = projected * lax.rsqrt(jnp.sum(projected * projected, axis=1, keepdims=True) + EPS)
    normed = normed.astype(jnp.bfloat16)
    for i in range(2):
        sent = jnp.dot(chosen[i], normed, preferred_element_type=jnp.float32)
        out_ref[:, i * width : (i + 1) * width] = sent.astype(jnp.bfloat16)


class Members:
    def __init__(self, ref, width, step):
        self.ref, self.width, self.step = ref, width, step

    def rows(self, index):
        span = slice(index // 2 * self.step, (index // 2 + 1) * self.step)
        return self.ref[span, index % 2 * self.width : (index % 2 + 1) * self.width]

    def weights(self, index, shape, dim):
        first = 2 * (index % 2)
        return bf16(jnp.where(iota(shape, dim) == first, 16, jnp.where(iota(shape, dim) == first + 1, 1, 0)))

    def digits(self, index):
        return self.ref[index // 2 * self.step : (index // 2 + 1) * self.step, 2 * self.width :]

    def down(self, index):
        weights = self.weights(index, (128, self.step), 0)
        return jnp.dot(self.digits(index), weights, preferred_element_type=jnp.float32)

    def along(self, index):
        weights = self.weights(index, (8, 128), 1)
        return lax.dot_general(weights, self.digits(index), NT, preferred_element_type=jnp.float32)[0:1]


def earlier_max(best, members, queries, numbers):
    splits, step = len(best), numbers[0].shape[1]
    for b in range(splits):
        rows = jnp.concatenate([part.rows(b) for part in members], axis=0)
        number = jnp.concatenate([part.down(b) for part in members], axis=0)
        number = jnp.where(number > 0, number, FAR)
        later = jnp.concatenate([queries.rows(a) for a in range(b, splits)], axis=0)
        scores = lax.dot_general(rows, later, NT, preferred_element_type=jnp.float32)
        for a in range(b, splits):
            found = jnp.where(number < numbers[a], scores[:, (a - b) * step : (a - b + 1) * step], -1.0)
            best[a] = jnp.maximum(best[a], jnp.max(found.reshape(-1, 8, step), axis=0))
    return best


def own_kernel(splits, width, step, own_ref, out_ref):
    own = Members(own_ref, width, step)
    best = [jnp.full((8, step), -1.0, jnp.float32) for _ in range(splits)]
    best = earlier_max(best, [own], own, [own.along(a) for a in range(splits)])
    for a in range(splits):
        out_ref[:, a * step : (a + 1) * step] = best[a]


def ring_kernel(splits, width, step, index_ref, owner_ref, size_ref, own_ref, left_ref, right_ref, best_ref, out_ref):
    block = out_ref.shape[2]
    own, left, right = [Members(ref, width, step) for ref in (own_ref, left_ref, right_ref)]
    own_best = [best_ref[:, a * step : (a + 1) * step] for a in range(splits)]
    own_best = earlier_max(own_best, [left, right], own, [own.along(a) for a in range(splits)])
    left_best = [jnp.full((8, step), -1.0, jnp.float32) for _ in range(splits)]
    left_best = earlier_max(left_best, [right], left, [left.along(a) for a in range(splits)])

    size = jnp.sum(jnp.where(owner_ref[...] == index_ref[0], size_ref[...], 0), axis=1, keepdims=True)
    for a in range(splits):
        rank = a * block + iota((1, block), 1)
        target = (rank + 1).astype(jnp.float32)
        column = jnp.concatenate([own.down(a), left.down(a)], axis=0)
        chosen = jnp.concatenate(
            [bf16(column == target[:, i * step : (i + 1) * step]) for i in range(block // step)], axis=1
        )
        best = jnp.concatenate(
            [jnp.max(own_best[a], axis=0, keepdims=True), jnp.max(left_best[a], axis=0, keepdims=True)], axis=1
        )
        first = best.astype(jnp.bfloat16)
        rest = best - first.astype(jnp.float32)
        second = rest.astype(jnp.bfloat16)
        third = (rest - second.astype(jnp.float32)).astype(jnp.bfloat16)
        line = iota((8, best.shape[1]), 0)
        terms = jnp.ones(line.shape, jnp.float32)
        for i, term in enumerate((first, second, third)):
            terms = jnp.where(line == i, term.astype(jnp.float32), terms)
        found = jnp.dot(terms.astype(jnp.bfloat16), chosen, preferred_element_type=jnp.float32)
        ordered = found[0:1] + found[1:2] + found[2:3]
        ordered = jnp.where((found[3:4] > 0) & (rank < size), ordered, -1.0)
        for i in range(splits):
            out_ref[i * splits + a] = jnp.where(index_ref[1] == i, ordered, -1.0)


def local(features, proj_weight, row_cluster, row_rank, owner_slot, tile_size):
    owners, splits = lax.axis_size("dp"), lax.axis_size("split")
    planes = owners // (2 * splits)
    rows, width = features.shape[0], proj_weight.shape[1]
    block = TILE // splits
    hbm = pl.BlockSpec(memory_space=pltpu.HBM)
    vmem = pl.BlockSpec(memory_space=pltpu.VMEM)
    smem = pl.BlockSpec(memory_space=pltpu.SMEM)
    params = pltpu.CompilerParams(vmem_limit_bytes=32 * 1024 * 1024)
    owner_row = owner_slot.reshape(1, -1)
    member = jnp.where(row_cluster >= 0, row_cluster * TILE + row_rank, -1)

    def device(z, y, core, x):
        return ((z * splits + y) * 2 + core) * splits + x

    everywhere = [(z, a, b) for z in range(planes) for a in range(splits) for b in range(splits)]
    diagonals = [
        [
            device(z, (g - j) % splits, 1, j) if core else device(z, j, 0, (g - j) % splits)
            for z in range(planes)
            for j in range(splits)
            for core in range(2)
        ]
        for g in range(splits)
    ]
    sheets = [
        [device(z, a, core, b) for a in range(splits) for b in range(splits)] for z in range(planes) for core in range(2)
    ]

    def shift(array, step):
        pairs = [(device(z, a, 0, b), device(z, a, 0, (b + step) % splits)) for z, a, b in everywhere]
        pairs += [(device(z, a, 1, b), device(z, (a + step) % splits, 1, b)) for z, a, b in everywhere]
        return lax.ppermute(array, AXES, pairs)

    outgoing = pl.pallas_call(
        lambda *refs: project_kernel(splits, block, *refs),
        out_shape=jax.ShapeDtypeStruct((rows // 2, 2 * width + 128), jnp.bfloat16),
        in_specs=[hbm] * 2 + [vmem] * 2,
        out_specs=vmem,
        scratch_shapes=[
            pltpu.VMEM(features.shape, jnp.bfloat16),
            pltpu.VMEM(proj_weight.shape, jnp.bfloat16),
            pltpu.SemaphoreType.DMA((8,)),
        ],
        compiler_params=pltpu.CompilerParams(vmem_limit_bytes=55200000),
        name="project",
    )(features, proj_weight, member.reshape(1, rows), owner_row)

    own = lax.all_to_all(
        outgoing.reshape(owners, splits // 2, -1), AXES, 0, 0, tiled=True, axis_index_groups=diagonals
    )
    own = own.transpose(1, 0, 2).reshape(rows // 2, -1)
    left, right = shift(own, 1), shift(own, -1)

    best = pl.pallas_call(
        lambda *refs: own_kernel(splits, width, owners, *refs),
        out_shape=jax.ShapeDtypeStruct((8, splits * owners), jnp.float32),
        in_specs=[vmem],
        out_specs=vmem,
        compiler_params=params,
        name="own",
        cost_estimate=pl.CostEstimate(flops=2 * rows * rows * width, bytes_accessed=2 << 20, transcendentals=0),
    )(own)
    owner, x = lax.axis_index("dp"), lax.axis_index("split")
    z, y, core = owner // (2 * splits), owner // 2 % splits, owner % 2
    line = jnp.where(core == 0, y, x)
    index = jnp.stack([(z * splits + line) * 2 + core, line]).astype(jnp.int32)
    best = pl.pallas_call(
        lambda *refs: ring_kernel(splits, width, owners, *refs),
        out_shape=jax.ShapeDtypeStruct((splits * splits, 1, block), jnp.float32),
        in_specs=[smem] + [vmem] * 6,
        out_specs=vmem,
        compiler_params=params,
        name="ring",
    )(index, owner_row, tile_size.reshape(1, -1), own, left, right, best)
    return jnp.max(lax.all_to_all(best, AXES, 0, 0, tiled=True, axis_index_groups=sheets), axis=0)


def solution(mesh):
    return jax.shard_map(
        local,
        mesh=mesh,
        in_specs=(P(("dp", "split"), None), P(), P(("dp", "split")), P(("dp", "split")), P(), P()),
        out_specs=P("dp", "split"),
        check_vma=False,
    )
```

```python
import jax
import jax.numpy as jnp
from jax import lax
from jax.experimental import pallas as pl
from jax.experimental.pallas import tpu as pltpu
from jax.sharding import PartitionSpec as P

TILE = 2048
EPS = 1e-06
AXES = ("dp", "split")
NT = (((1,), (1,)), ((), ()))
FAR = 1e9


def iota(shape, dim):
    return lax.broadcasted_iota(jnp.int32, shape, dim)


def bf16(mask_or_int):
    return mask_or_int.astype(jnp.float32).astype(jnp.bfloat16)


def project_kernel(
    splits, block, features_hbm, weight_hbm, member_ref, owner_ref, other_ref, mine_ref, features, weight, semaphores
):
    steps = 4
    part = features.shape[1] // steps
    spans = [slice(i * part, (i + 1) * part) for i in range(steps)]
    pairs = []
    for span in spans:
        pairs.append((weight_hbm.at[span, :], weight.at[span, :]))
        pairs.append((features_hbm.at[:, span], features.at[:, span]))
    copies = [pltpu.make_async_copy(*pair, semaphores.at[i]) for i, pair in enumerate(pairs)]
    for copy in copies:
        copy.start()
    member = member_ref[...]
    clusters, rows, width = owner_ref.shape[1], member.shape[1], weight.shape[1]
    chips = mine_ref.shape[0]
    cluster, rank = member // TILE, member % TILE
    owner = bf16(jnp.broadcast_to(owner_ref[...], (8, clusters)))
    named = bf16(iota((clusters, rows), 0) == cluster)
    slot = jnp.dot(owner, named, preferred_element_type=jnp.float32)[0:1].astype(jnp.int32)
    core = lax.axis_index("dp") % 2
    place = rank // block * chips + slot // 2
    high, low = (rank + 1) // 16, (rank + 1) % 16
    lane = iota((128, rows), 0)
    digits = bf16(jnp.where(lane // 2 == rank // block, jnp.where(lane % 2 == 0, high, low), 0))
    outs = []
    for out_ref, to in ((other_ref, 1 - core), (mine_ref, core)):
        target = jnp.where((member >= 0) & (slot % 2 == to), place, -1)
        chosen = bf16(iota((splits * chips, rows), 0) == target)
        outs.append((out_ref, chosen))
        anywhere = chosen[:chips]
        for a in range(1, splits):
            anywhere = anywhere + chosen[a * chips : (a + 1) * chips]
        numbers = lax.dot_general(anywhere, digits, NT, preferred_element_type=jnp.float32)
        out_ref[:, splits * width :] = numbers.astype(jnp.bfloat16)

    projected = jnp.zeros((rows, width), jnp.float32)
    for i, span in enumerate(spans):
        copies[2 * i].wait()
        copies[2 * i + 1].wait()
        projected += jnp.dot(features[:, span], weight[span, :], preferred_element_type=jnp.float32)
    normed = projected * lax.rsqrt(jnp.sum(projected * projected, axis=1, keepdims=True) + EPS)
    normed = normed.astype(jnp.bfloat16)
    for out_ref, chosen in outs:
        sent = jnp.dot(chosen, normed, preferred_element_type=jnp.float32).astype(jnp.bfloat16)
        for a in range(splits):
            out_ref[:, a * width : (a + 1) * width] = sent[a * chips : (a + 1) * chips]


def merge_kernel(first_ref, second_ref, out_ref):
    out_ref[:, 0, :] = first_ref[...]
    out_ref[:, 1, :] = second_ref[...]


class Members:
    def __init__(self, ref, width, splits):
        self.ref, self.width, self.splits, self.digits = ref, width, splits, ref[:, splits * width :]

    def rows(self, index):
        return self.ref[:, index * self.width : (index + 1) * self.width]

    def down(self):
        step = self.ref.shape[0]
        lane, digit = iota((128, self.splits * step), 1) // step, iota((128, self.splits * step), 0)
        weights = bf16(jnp.where(digit == 2 * lane, 16, jnp.where(digit == 2 * lane + 1, 1, 0)))
        return jnp.dot(self.digits, weights, preferred_element_type=jnp.float32)

    def along(self):
        line, digit = iota((8, 128), 0), iota((8, 128), 1)
        weights = bf16(jnp.where(digit == 2 * line, 16, jnp.where(digit == 2 * line + 1, 1, 0)))
        return lax.dot_general(weights, self.digits, NT, preferred_element_type=jnp.float32)

    def stacked(self):
        return jnp.concatenate([self.rows(a) for a in range(self.splits)], axis=0)


def earlier_max(best, members, queries):
    splits, step = len(best), queries.ref.shape[0]
    later, numbers = queries.stacked(), queries.along()
    for part in members:
        scores = lax.dot_general(part.stacked(), later, NT, preferred_element_type=jnp.float32)
        down = part.down()
        down = jnp.where(down > 0, down, FAR)
        for b in range(splits):
            number = down[:, b * step : (b + 1) * step]
            for a in range(b, splits):
                tile = scores[b * step : (b + 1) * step, a * step : (a + 1) * step]
                found = jnp.where(number < numbers[a : a + 1], tile, -1.0)
                best[a] = jnp.maximum(best[a], jnp.max(found.reshape(-1, 8, step), axis=0))
    return best


def own_kernel(splits, width, step, own_ref, out_ref):
    own = Members(own_ref, width, splits)
    best = [jnp.full((8, step), -1.0, jnp.float32) for _ in range(splits)]
    best = earlier_max(best, [own], own)
    for a in range(splits):
        out_ref[:, a * step : (a + 1) * step] = best[a]


def ring_kernel(splits, width, step, index_ref, owner_ref, size_ref, own_ref, left_ref, right_ref, best_ref, out_ref):
    block = out_ref.shape[2]
    own, left, right = [Members(ref, width, splits) for ref in (own_ref, left_ref, right_ref)]
    own_best = [best_ref[:, a * step : (a + 1) * step] for a in range(splits)]
    own_best = earlier_max(own_best, [left, right], own)
    left_best = [jnp.full((8, step), -1.0, jnp.float32) for _ in range(splits)]
    left_best = earlier_max(left_best, [right], left)
    own_down, left_down = own.down(), left.down()

    size = jnp.sum(jnp.where(owner_ref[...] == index_ref[0], size_ref[...], 0), axis=1, keepdims=True)
    for a in range(splits):
        rank = a * block + iota((1, block), 1)
        target = (rank + 1).astype(jnp.float32)
        span = slice(a * step, (a + 1) * step)
        column = jnp.concatenate([own_down[:, span], left_down[:, span]], axis=0)
        chosen = jnp.concatenate(
            [bf16(column == target[:, i * step : (i + 1) * step]) for i in range(block // step)], axis=1
        )
        best = jnp.concatenate(
            [jnp.max(own_best[a], axis=0, keepdims=True), jnp.max(left_best[a], axis=0, keepdims=True)], axis=1
        )
        first = best.astype(jnp.bfloat16)
        rest = best - first.astype(jnp.float32)
        second = rest.astype(jnp.bfloat16)
        third = (rest - second.astype(jnp.float32)).astype(jnp.bfloat16)
        line = iota((8, best.shape[1]), 0)
        terms = jnp.ones(line.shape, jnp.float32)
        for i, term in enumerate((first, second, third)):
            terms = jnp.where(line == i, term.astype(jnp.float32), terms)
        found = jnp.dot(terms.astype(jnp.bfloat16), chosen, preferred_element_type=jnp.float32)
        ordered = found[0:1] + found[1:2] + found[2:3]
        ordered = jnp.where((found[3:4] > 0) & (rank < size), ordered, -1.0)
        for i in range(splits):
            out_ref[i * splits + a] = jnp.where(index_ref[1] == i, ordered, -1.0)


def local(features, proj_weight, row_cluster, row_rank, owner_slot, tile_size):
    owners, splits = lax.axis_size("dp"), lax.axis_size("split")
    planes = owners // (2 * splits)
    rows, width = features.shape[0], proj_weight.shape[1]
    block = TILE // splits
    hbm = pl.BlockSpec(memory_space=pltpu.HBM)
    vmem = pl.BlockSpec(memory_space=pltpu.VMEM)
    smem = pl.BlockSpec(memory_space=pltpu.SMEM)
    params = pltpu.CompilerParams(vmem_limit_bytes=32 * 1024 * 1024)
    owner_row = owner_slot.reshape(1, -1)
    member = jnp.where(row_cluster >= 0, row_cluster * TILE + row_rank, -1)

    def device(z, y, core, x):
        return ((z * splits + y) * 2 + core) * splits + x

    everywhere = [(z, a, b) for z in range(planes) for a in range(splits) for b in range(splits)]
    columns = [[device(z, j, 0, g) for z in range(planes) for j in range(splits)] for g in range(splits)]
    columns += [[device(z, g, 1, j) for z in range(planes) for j in range(splits)] for g in range(splits)]
    sheets = [
        [device(z, a, core, b) for a in range(splits) for b in range(splits)] for z in range(planes) for core in range(2)
    ]

    def shift(array, step):
        pairs = [(device(z, a, 0, b), device(z, a, 0, (b + step) % splits)) for z, a, b in everywhere]
        pairs += [(device(z, a, 1, b), device(z, (a + step) % splits, 1, b)) for z, a, b in everywhere]
        return lax.ppermute(array, AXES, pairs)

    chips = owners // 2
    other, mine = pl.pallas_call(
        lambda *refs: project_kernel(splits, block, *refs),
        out_shape=[jax.ShapeDtypeStruct((chips, splits * width + 128), jnp.bfloat16)] * 2,
        in_specs=[hbm] * 2 + [vmem] * 2,
        out_specs=[vmem] * 2,
        scratch_shapes=[
            pltpu.VMEM(features.shape, jnp.bfloat16),
            pltpu.VMEM(proj_weight.shape, jnp.bfloat16),
            pltpu.SemaphoreType.DMA((8,)),
        ],
        compiler_params=pltpu.CompilerParams(vmem_limit_bytes=55200000),
        name="project",
    )(features, proj_weight, member.reshape(1, rows), owner_row)

    swap = [(device(z, a, core, b), device(z, a, 1 - core, b)) for z, a, b in everywhere for core in range(2)]
    outgoing = pl.pallas_call(
        merge_kernel,
        out_shape=jax.ShapeDtypeStruct((chips, 2, splits * width + 128), jnp.bfloat16),
        in_specs=[vmem] * 2,
        out_specs=vmem,
        compiler_params=params,
        name="merge",
    )(mine, lax.ppermute(other, AXES, swap))
    own = lax.all_to_all(outgoing, AXES, 0, 0, tiled=True, axis_index_groups=columns).reshape(owners, -1)
    left, right = shift(own, 1), shift(own, -1)

    best = pl.pallas_call(
        lambda *refs: own_kernel(splits, width, owners, *refs),
        out_shape=jax.ShapeDtypeStruct((8, splits * owners), jnp.float32),
        in_specs=[vmem],
        out_specs=vmem,
        compiler_params=params,
        name="own",
        cost_estimate=pl.CostEstimate(flops=2 * rows * rows * width, bytes_accessed=2 << 20, transcendentals=0),
    )(own)
    owner, x = lax.axis_index("dp"), lax.axis_index("split")
    z, y, core = owner // (2 * splits), owner // 2 % splits, owner % 2
    line = jnp.where(core == 0, y, x)
    index = jnp.stack([(z * splits + line) * 2 + core, line]).astype(jnp.int32)
    best = pl.pallas_call(
        lambda *refs: ring_kernel(splits, width, owners, *refs),
        out_shape=jax.ShapeDtypeStruct((splits * splits, 1, block), jnp.float32),
        in_specs=[smem] + [vmem] * 6,
        out_specs=vmem,
        compiler_params=params,
        name="ring",
    )(index, owner_row, tile_size.reshape(1, -1), own, left, right, best)
    return jnp.max(lax.all_to_all(best, AXES, 0, 0, tiled=True, axis_index_groups=sheets), axis=0)


def solution(mesh):
    return jax.shard_map(
        local,
        mesh=mesh,
        in_specs=(P(("dp", "split"), None), P(), P(("dp", "split")), P(("dp", "split")), P(), P()),
        out_specs=P("dp", "split"),
        check_vma=False,
    )
```

```python
import jax
import jax.numpy as jnp
from jax import lax
from jax.experimental import pallas as pl
from jax.experimental.pallas import tpu as pltpu
from jax.sharding import PartitionSpec as P

TILE = 2048
EPS = 1e-06
AXES = ("dp", "split")
NT = (((1,), (1,)), ((), ()))
FAR = 1e9


def iota(shape, dim):
    return lax.broadcasted_iota(jnp.int32, shape, dim)


def bf16(mask_or_int):
    return mask_or_int.astype(jnp.float32).astype(jnp.bfloat16)


def project_kernel(
    splits, block, features_hbm, weight_hbm, member_ref, owner_ref, other_ref, mine_ref, features, weight, semaphores
):
    steps = 4
    part = features.shape[1] // steps
    spans = [slice(i * part, (i + 1) * part) for i in range(steps)]
    pairs = []
    for span in spans:
        pairs.append((weight_hbm.at[span, :], weight.at[span, :]))
        pairs.append((features_hbm.at[:, span], features.at[:, span]))
    copies = [pltpu.make_async_copy(*pair, semaphores.at[i]) for i, pair in enumerate(pairs)]
    for copy in copies:
        copy.start()
    member = member_ref[...]
    clusters, rows, width = owner_ref.shape[1], member.shape[1], weight.shape[1]
    chips = mine_ref.shape[0]
    cluster, rank = member // TILE, member % TILE
    owner = bf16(jnp.broadcast_to(owner_ref[...], (8, clusters)))
    named = bf16(iota((clusters, rows), 0) == cluster)
    slot = jnp.dot(owner, named, preferred_element_type=jnp.float32)[0:1].astype(jnp.int32)
    core = lax.axis_index("dp") % 2
    here = jnp.where(slot % 2 == core, 1, 0)
    target = jnp.where(member >= 0, (here * splits + rank // block) * chips + slot // 2, -1)
    chosen = bf16(iota((2 * splits * chips, rows), 0) == target)
    high, low = (rank + 1) // 16, (rank + 1) % 16
    lane = iota((128, rows), 0)
    digits = bf16(jnp.where(lane // 2 == rank // block, jnp.where(lane % 2 == 0, high, low), 0))
    for i, out_ref in enumerate((other_ref, mine_ref)):
        parts = [chosen[(i * splits + a) * chips : (i * splits + a + 1) * chips] for a in range(splits)]
        anywhere = (parts[0] + parts[1]) + (parts[2] + parts[3])
        numbers = lax.dot_general(anywhere, digits, NT, preferred_element_type=jnp.float32)
        out_ref[:, splits * width :] = numbers.astype(jnp.bfloat16)

    projected = jnp.zeros((rows, width), jnp.float32)
    for i, span in enumerate(spans):
        copies[2 * i].wait()
        copies[2 * i + 1].wait()
        projected += jnp.dot(features[:, span], weight[span, :], preferred_element_type=jnp.float32)
    normed = projected * lax.rsqrt(jnp.sum(projected * projected, axis=1, keepdims=True) + EPS)
    normed = normed.astype(jnp.bfloat16)
    sent = jnp.dot(chosen, normed, preferred_element_type=jnp.float32).astype(jnp.bfloat16)
    for i, out_ref in enumerate((other_ref, mine_ref)):
        for a in range(splits):
            start = (i * splits + a) * chips
            out_ref[:, a * width : (a + 1) * width] = sent[start : start + chips]


def merge_kernel(first_ref, second_ref, out_ref):
    out_ref[:, 0, :] = first_ref[...]
    out_ref[:, 1, :] = second_ref[...]


class Members:
    def __init__(self, ref, width, splits):
        self.ref, self.width, self.splits, self.digits = ref, width, splits, ref[:, splits * width :]

    def rows(self, index):
        return self.ref[:, index * self.width : (index + 1) * self.width]

    def down(self):
        step = self.ref.shape[0]
        lane, digit = iota((128, self.splits * step), 1) // step, iota((128, self.splits * step), 0)
        weights = bf16(jnp.where(digit == 2 * lane, 16, jnp.where(digit == 2 * lane + 1, 1, 0)))
        return jnp.dot(self.digits, weights, preferred_element_type=jnp.float32)

    def along(self):
        line, digit = iota((8, 128), 0), iota((8, 128), 1)
        weights = bf16(jnp.where(digit == 2 * line, 16, jnp.where(digit == 2 * line + 1, 1, 0)))
        return lax.dot_general(weights, self.digits, NT, preferred_element_type=jnp.float32)

    def stacked(self):
        return jnp.concatenate([self.rows(a) for a in range(self.splits)], axis=0)


def earlier_max(best, members, queries):
    splits, step = len(best), queries.ref.shape[0]
    later, numbers = queries.stacked(), queries.along()
    for part in members:
        scores = lax.dot_general(part.stacked(), later, NT, preferred_element_type=jnp.float32)
        down = part.down()
        down = jnp.where(down > 0, down, FAR)
        for b in range(splits):
            number = down[:, b * step : (b + 1) * step]
            for a in range(b, splits):
                tile = scores[b * step : (b + 1) * step, a * step : (a + 1) * step]
                found = jnp.where(number < numbers[a : a + 1], tile, -1.0)
                best[a] = jnp.maximum(best[a], jnp.max(found.reshape(-1, 8, step), axis=0))
    return best


def own_kernel(splits, width, step, own_ref, out_ref):
    own = Members(own_ref, width, splits)
    best = [jnp.full((8, step), -1.0, jnp.float32) for _ in range(splits)]
    best = earlier_max(best, [own], own)
    for a in range(splits):
        out_ref[:, a * step : (a + 1) * step] = best[a]


def side_kernel(splits, width, step, own_ref, side_ref, best_ref, out_ref):
    own, side = [Members(ref, width, splits) for ref in (own_ref, side_ref)]
    best = earlier_max([best_ref[:, a * step : (a + 1) * step] for a in range(splits)], [side], own)
    for a in range(splits):
        out_ref[:, a * step : (a + 1) * step] = best[a]


def ring_kernel(splits, width, step, index_ref, owner_ref, size_ref, own_ref, left_ref, right_ref, best_ref, out_ref):
    block = out_ref.shape[2]
    own, left, right = [Members(ref, width, splits) for ref in (own_ref, left_ref, right_ref)]
    own_best = [best_ref[:, a * step : (a + 1) * step] for a in range(splits)]
    own_best = earlier_max(own_best, [left], own)
    left_best = [jnp.full((8, step), -1.0, jnp.float32) for _ in range(splits)]
    left_best = earlier_max(left_best, [right], left)
    own_down, left_down = own.down(), left.down()

    size = jnp.sum(jnp.where(owner_ref[...] == index_ref[0], size_ref[...], 0), axis=1, keepdims=True)
    for a in range(splits):
        rank = a * block + iota((1, block), 1)
        target = (rank + 1).astype(jnp.float32)
        span = slice(a * step, (a + 1) * step)
        column = jnp.concatenate([own_down[:, span], left_down[:, span]], axis=0)
        chosen = jnp.concatenate(
            [bf16(column == target[:, i * step : (i + 1) * step]) for i in range(block // step)], axis=1
        )
        best = jnp.concatenate(
            [jnp.max(own_best[a], axis=0, keepdims=True), jnp.max(left_best[a], axis=0, keepdims=True)], axis=1
        )
        first = best.astype(jnp.bfloat16)
        rest = best - first.astype(jnp.float32)
        second = rest.astype(jnp.bfloat16)
        third = (rest - second.astype(jnp.float32)).astype(jnp.bfloat16)
        line = iota((8, best.shape[1]), 0)
        terms = jnp.ones(line.shape, jnp.float32)
        for i, term in enumerate((first, second, third)):
            terms = jnp.where(line == i, term.astype(jnp.float32), terms)
        found = jnp.dot(terms.astype(jnp.bfloat16), chosen, preferred_element_type=jnp.float32)
        ordered = found[0:1] + found[1:2] + found[2:3]
        ordered = jnp.where((found[3:4] > 0) & (rank < size), ordered, -1.0)
        for i in range(splits):
            out_ref[i * splits + a] = jnp.where(index_ref[1] == i, ordered, -1.0)


def local(features, proj_weight, row_cluster, row_rank, owner_slot, tile_size):
    owners, splits = lax.axis_size("dp"), lax.axis_size("split")
    planes = owners // (2 * splits)
    rows, width = features.shape[0], proj_weight.shape[1]
    block = TILE // splits
    hbm = pl.BlockSpec(memory_space=pltpu.HBM)
    vmem = pl.BlockSpec(memory_space=pltpu.VMEM)
    smem = pl.BlockSpec(memory_space=pltpu.SMEM)
    params = pltpu.CompilerParams(vmem_limit_bytes=32 * 1024 * 1024)
    owner_row = owner_slot.reshape(1, -1)
    member = jnp.where(row_cluster >= 0, row_cluster * TILE + row_rank, -1)

    def device(z, y, core, x):
        return ((z * splits + y) * 2 + core) * splits + x

    everywhere = [(z, a, b) for z in range(planes) for a in range(splits) for b in range(splits)]
    columns = [[device(z, j, 0, g) for z in range(planes) for j in range(splits)] for g in range(splits)]
    columns += [[device(z, g, 1, j) for z in range(planes) for j in range(splits)] for g in range(splits)]
    sheets = [
        [device(z, a, core, b) for a in range(splits) for b in range(splits)] for z in range(planes) for core in range(2)
    ]

    def shift(array, step):
        pairs = [(device(z, a, 0, b), device(z, a, 0, (b + step) % splits)) for z, a, b in everywhere]
        pairs += [(device(z, a, 1, b), device(z, (a + step) % splits, 1, b)) for z, a, b in everywhere]
        return lax.ppermute(array, AXES, pairs)

    chips = owners // 2
    other, mine = pl.pallas_call(
        lambda *refs: project_kernel(splits, block, *refs),
        out_shape=[jax.ShapeDtypeStruct((chips, splits * width + 128), jnp.bfloat16)] * 2,
        in_specs=[hbm] * 2 + [vmem] * 2,
        out_specs=[vmem] * 2,
        scratch_shapes=[
            pltpu.VMEM(features.shape, jnp.bfloat16),
            pltpu.VMEM(proj_weight.shape, jnp.bfloat16),
            pltpu.SemaphoreType.DMA((8,)),
        ],
        compiler_params=pltpu.CompilerParams(vmem_limit_bytes=55200000),
        name="project",
    )(features, proj_weight, member.reshape(1, rows), owner_row)

    swap = [(device(z, a, core, b), device(z, a, 1 - core, b)) for z, a, b in everywhere for core in range(2)]
    outgoing = pl.pallas_call(
        merge_kernel,
        out_shape=jax.ShapeDtypeStruct((chips, 2, splits * width + 128), jnp.bfloat16),
        in_specs=[vmem] * 2,
        out_specs=vmem,
        compiler_params=params,
        name="merge",
    )(mine, lax.ppermute(other, AXES, swap))
    own = lax.all_to_all(outgoing, AXES, 0, 0, tiled=True, axis_index_groups=columns).reshape(owners, -1)
    left, right = shift(own, 1), shift(own, -1)

    best = pl.pallas_call(
        lambda *refs: own_kernel(splits, width, owners, *refs),
        out_shape=jax.ShapeDtypeStruct((8, splits * owners), jnp.float32),
        in_specs=[vmem],
        out_specs=vmem,
        compiler_params=params,
        name="own",
        cost_estimate=pl.CostEstimate(flops=2 * rows * rows * width, bytes_accessed=2 << 20, transcendentals=0),
    )(own)
    best = pl.pallas_call(
        lambda *refs: side_kernel(splits, width, owners, *refs),
        out_shape=jax.ShapeDtypeStruct((8, splits * owners), jnp.float32),
        in_specs=[vmem] * 3,
        out_specs=vmem,
        compiler_params=params,
        name="side",
        cost_estimate=pl.CostEstimate(flops=2 * rows * rows * width, bytes_accessed=2 << 20, transcendentals=0),
    )(own, right, best)
    owner, x = lax.axis_index("dp"), lax.axis_index("split")
    z, y, core = owner // (2 * splits), owner // 2 % splits, owner % 2
    line = jnp.where(core == 0, y, x)
    index = jnp.stack([(z * splits + line) * 2 + core, line]).astype(jnp.int32)
    best = pl.pallas_call(
        lambda *refs: ring_kernel(splits, width, owners, *refs),
        out_shape=jax.ShapeDtypeStruct((splits * splits, 1, block), jnp.float32),
        in_specs=[smem] + [vmem] * 6,
        out_specs=vmem,
        compiler_params=params,
        name="ring",
    )(index, owner_row, tile_size.reshape(1, -1), own, left, right, best)
    return jnp.max(lax.all_to_all(best, AXES, 0, 0, tiled=True, axis_index_groups=sheets), axis=0)


def solution(mesh):
    return jax.shard_map(
        local,
        mesh=mesh,
        in_specs=(P(("dp", "split"), None), P(), P(("dp", "split")), P(("dp", "split")), P(), P()),
        out_specs=P("dp", "split"),
        check_vma=False,
    )
```

```python
import jax
import jax.numpy as jnp
from jax import lax
from jax.experimental import pallas as pl
from jax.experimental.pallas import tpu as pltpu
from jax.sharding import PartitionSpec as P

TILE = 2048
EPS = 1e-06
AXES = ("dp", "split")
NT = (((1,), (1,)), ((), ()))
FAR = 1e9


def plane_order(planes):
    bits = max(planes.bit_length() - 1, 0)
    if planes != 1 << bits:
        return list(range(planes))
    return [sum((z >> i & 1) << bits - 1 - i for i in range(bits)) for z in range(planes)]


def iota(shape, dim):
    return lax.broadcasted_iota(jnp.int32, shape, dim)


def bf16(mask_or_int):
    return mask_or_int.astype(jnp.float32).astype(jnp.bfloat16)


def project_kernel(
    splits, block, features_hbm, weight_hbm, member_ref, owner_ref, other_ref, mine_ref, features, weight, semaphores
):
    steps = 4
    part = features.shape[1] // steps
    spans = [slice(i * part, (i + 1) * part) for i in range(steps)]
    pairs = []
    for span in spans:
        pairs.append((weight_hbm.at[span, :], weight.at[span, :]))
        pairs.append((features_hbm.at[:, span], features.at[:, span]))
    copies = [pltpu.make_async_copy(*pair, semaphores.at[i]) for i, pair in enumerate(pairs)]
    for copy in copies:
        copy.start()
    member = member_ref[...]
    clusters, rows, width = owner_ref.shape[1], member.shape[1], weight.shape[1]
    chips = mine_ref.shape[0]
    cluster, rank = member // TILE, member % TILE
    owner = bf16(jnp.broadcast_to(owner_ref[...], (8, clusters)))
    named = bf16(iota((clusters, rows), 0) == cluster)
    slot = jnp.dot(owner, named, preferred_element_type=jnp.float32)[0:1].astype(jnp.int32)
    core = lax.axis_index("dp") % 2
    here = jnp.where(slot % 2 == core, 1, 0)
    chip = jnp.zeros_like(slot)
    for i, z in enumerate(plane_order(chips // splits)):
        chip = jnp.where(slot // (2 * splits) == z, i * splits + slot // 2 % splits, chip)
    target = jnp.where(member >= 0, (here * splits + rank // block) * chips + chip, -1)
    chosen = bf16(iota((2 * splits * chips, rows), 0) == target)
    high, low = (rank + 1) // 16, (rank + 1) % 16
    lane = iota((128, rows), 0)
    digits = bf16(jnp.where(lane // 2 == rank // block, jnp.where(lane % 2 == 0, high, low), 0))
    for i, out_ref in enumerate((other_ref, mine_ref)):
        parts = [chosen[(i * splits + a) * chips : (i * splits + a + 1) * chips] for a in range(splits)]
        anywhere = (parts[0] + parts[1]) + (parts[2] + parts[3])
        numbers = lax.dot_general(anywhere, digits, NT, preferred_element_type=jnp.float32)
        out_ref[:, splits * width :] = numbers.astype(jnp.bfloat16)

    projected = jnp.zeros((rows, width), jnp.float32)
    for i, span in enumerate(spans):
        copies[2 * i].wait()
        copies[2 * i + 1].wait()
        projected += jnp.dot(features[:, span], weight[span, :], preferred_element_type=jnp.float32)
    normed = projected * lax.rsqrt(jnp.sum(projected * projected, axis=1, keepdims=True) + EPS)
    normed = normed.astype(jnp.bfloat16)
    sent = jnp.dot(chosen, normed, preferred_element_type=jnp.float32).astype(jnp.bfloat16)
    for i, out_ref in enumerate((other_ref, mine_ref)):
        for a in range(splits):
            start = (i * splits + a) * chips
            out_ref[:, a * width : (a + 1) * width] = sent[start : start + chips]


def merge_kernel(first_ref, second_ref, out_ref):
    out_ref[:, 0, :] = first_ref[...]
    out_ref[:, 1, :] = second_ref[...]


class Members:
    def __init__(self, ref, width, splits):
        self.ref, self.width, self.splits, self.digits = ref, width, splits, ref[:, splits * width :]

    def rows(self, index):
        return self.ref[:, index * self.width : (index + 1) * self.width]

    def down(self):
        step = self.ref.shape[0]
        lane, digit = iota((128, self.splits * step), 1) // step, iota((128, self.splits * step), 0)
        weights = bf16(jnp.where(digit == 2 * lane, 16, jnp.where(digit == 2 * lane + 1, 1, 0)))
        return jnp.dot(self.digits, weights, preferred_element_type=jnp.float32)

    def along(self):
        line, digit = iota((8, 128), 0), iota((8, 128), 1)
        weights = bf16(jnp.where(digit == 2 * line, 16, jnp.where(digit == 2 * line + 1, 1, 0)))
        return lax.dot_general(weights, self.digits, NT, preferred_element_type=jnp.float32)

    def stacked(self):
        return jnp.concatenate([self.rows(a) for a in range(self.splits)], axis=0)


def earlier_max(best, members, queries):
    splits, step = len(best), queries.ref.shape[0]
    later, numbers = queries.stacked(), queries.along()
    for part in members:
        scores = lax.dot_general(part.stacked(), later, NT, preferred_element_type=jnp.float32)
        down = part.down()
        down = jnp.where(down > 0, down, FAR)
        for b in range(splits):
            number = down[:, b * step : (b + 1) * step]
            for a in range(b, splits):
                tile = scores[b * step : (b + 1) * step, a * step : (a + 1) * step]
                found = jnp.where(number < numbers[a : a + 1], tile, -1.0)
                best[a] = jnp.maximum(best[a], jnp.max(found.reshape(-1, 8, step), axis=0))
    return best


def own_kernel(splits, width, step, own_ref, out_ref):
    own = Members(own_ref, width, splits)
    best = [jnp.full((8, step), -1.0, jnp.float32) for _ in range(splits)]
    best = earlier_max(best, [own], own)
    for a in range(splits):
        out_ref[:, a * step : (a + 1) * step] = best[a]


def side_kernel(splits, width, step, own_ref, side_ref, best_ref, out_ref):
    own, side = [Members(ref, width, splits) for ref in (own_ref, side_ref)]
    best = earlier_max([best_ref[:, a * step : (a + 1) * step] for a in range(splits)], [side], own)
    for a in range(splits):
        out_ref[:, a * step : (a + 1) * step] = best[a]


def ring_kernel(splits, width, step, index_ref, owner_ref, size_ref, own_ref, left_ref, right_ref, best_ref, out_ref):
    block = out_ref.shape[2]
    own, left, right = [Members(ref, width, splits) for ref in (own_ref, left_ref, right_ref)]
    own_best = [best_ref[:, a * step : (a + 1) * step] for a in range(splits)]
    own_best = earlier_max(own_best, [left], own)
    left_best = [jnp.full((8, step), -1.0, jnp.float32) for _ in range(splits)]
    left_best = earlier_max(left_best, [right], left)
    own_down, left_down = own.down(), left.down()

    size = jnp.sum(jnp.where(owner_ref[...] == index_ref[0], size_ref[...], 0), axis=1, keepdims=True)
    for a in range(splits):
        rank = a * block + iota((1, block), 1)
        target = (rank + 1).astype(jnp.float32)
        span = slice(a * step, (a + 1) * step)
        column = jnp.concatenate([own_down[:, span], left_down[:, span]], axis=0)
        chosen = jnp.concatenate(
            [bf16(column == target[:, i * step : (i + 1) * step]) for i in range(block // step)], axis=1
        )
        best = jnp.concatenate(
            [jnp.max(own_best[a], axis=0, keepdims=True), jnp.max(left_best[a], axis=0, keepdims=True)], axis=1
        )
        first = best.astype(jnp.bfloat16)
        rest = best - first.astype(jnp.float32)
        second = rest.astype(jnp.bfloat16)
        third = (rest - second.astype(jnp.float32)).astype(jnp.bfloat16)
        line = iota((8, best.shape[1]), 0)
        terms = jnp.ones(line.shape, jnp.float32)
        for i, term in enumerate((first, second, third)):
            terms = jnp.where(line == i, term.astype(jnp.float32), terms)
        found = jnp.dot(terms.astype(jnp.bfloat16), chosen, preferred_element_type=jnp.float32)
        ordered = found[0:1] + found[1:2] + found[2:3]
        ordered = jnp.where((found[3:4] > 0) & (rank < size), ordered, -1.0)
        for i in range(splits):
            out_ref[i * splits + a] = jnp.where(index_ref[1] == i, ordered, -1.0)


def local(features, proj_weight, row_cluster, row_rank, owner_slot, tile_size):
    owners, splits = lax.axis_size("dp"), lax.axis_size("split")
    planes = owners // (2 * splits)
    rows, width = features.shape[0], proj_weight.shape[1]
    block = TILE // splits
    hbm = pl.BlockSpec(memory_space=pltpu.HBM)
    vmem = pl.BlockSpec(memory_space=pltpu.VMEM)
    smem = pl.BlockSpec(memory_space=pltpu.SMEM)
    params = pltpu.CompilerParams(vmem_limit_bytes=32 * 1024 * 1024)
    owner_row = owner_slot.reshape(1, -1)
    member = jnp.where(row_cluster >= 0, row_cluster * TILE + row_rank, -1)

    def device(z, y, core, x):
        return ((z * splits + y) * 2 + core) * splits + x

    everywhere = [(z, a, b) for z in range(planes) for a in range(splits) for b in range(splits)]
    order = plane_order(planes)
    columns = [[device(z, j, 0, g) for z in order for j in range(splits)] for g in range(splits)]
    columns += [[device(z, g, 1, j) for z in order for j in range(splits)] for g in range(splits)]
    sheets = [
        [device(z, a, core, b) for a in range(splits) for b in range(splits)] for z in range(planes) for core in range(2)
    ]

    def shift(array, step):
        pairs = [(device(z, a, 0, b), device(z, a, 0, (b + step) % splits)) for z, a, b in everywhere]
        pairs += [(device(z, a, 1, b), device(z, (a + step) % splits, 1, b)) for z, a, b in everywhere]
        return lax.ppermute(array, AXES, pairs)

    chips = owners // 2
    other, mine = pl.pallas_call(
        lambda *refs: project_kernel(splits, block, *refs),
        out_shape=[jax.ShapeDtypeStruct((chips, splits * width + 128), jnp.bfloat16)] * 2,
        in_specs=[hbm] * 2 + [vmem] * 2,
        out_specs=[vmem] * 2,
        scratch_shapes=[
            pltpu.VMEM(features.shape, jnp.bfloat16),
            pltpu.VMEM(proj_weight.shape, jnp.bfloat16),
            pltpu.SemaphoreType.DMA((8,)),
        ],
        compiler_params=pltpu.CompilerParams(vmem_limit_bytes=55200000),
        name="project",
    )(features, proj_weight, member.reshape(1, rows), owner_row)

    swap = [(device(z, a, core, b), device(z, a, 1 - core, b)) for z, a, b in everywhere for core in range(2)]
    outgoing = pl.pallas_call(
        merge_kernel,
        out_shape=jax.ShapeDtypeStruct((chips, 2, splits * width + 128), jnp.bfloat16),
        in_specs=[vmem] * 2,
        out_specs=vmem,
        compiler_params=params,
        name="merge",
    )(mine, lax.ppermute(other, AXES, swap))
    own = lax.all_to_all(outgoing, AXES, 0, 0, tiled=True, axis_index_groups=columns).reshape(owners, -1)
    left, right = shift(own, 1), shift(own, -1)

    best = pl.pallas_call(
        lambda *refs: own_kernel(splits, width, owners, *refs),
        out_shape=jax.ShapeDtypeStruct((8, splits * owners), jnp.float32),
        in_specs=[vmem],
        out_specs=vmem,
        compiler_params=params,
        name="own",
        cost_estimate=pl.CostEstimate(flops=2 * rows * rows * width, bytes_accessed=2 << 20, transcendentals=0),
    )(own)
    best = pl.pallas_call(
        lambda *refs: side_kernel(splits, width, owners, *refs),
        out_shape=jax.ShapeDtypeStruct((8, splits * owners), jnp.float32),
        in_specs=[vmem] * 3,
        out_specs=vmem,
        compiler_params=params,
        name="side",
        cost_estimate=pl.CostEstimate(flops=2 * rows * rows * width, bytes_accessed=2 << 20, transcendentals=0),
    )(own, right, best)
    owner, x = lax.axis_index("dp"), lax.axis_index("split")
    z, y, core = owner // (2 * splits), owner // 2 % splits, owner % 2
    line = jnp.where(core == 0, y, x)
    index = jnp.stack([(z * splits + line) * 2 + core, line]).astype(jnp.int32)
    best = pl.pallas_call(
        lambda *refs: ring_kernel(splits, width, owners, *refs),
        out_shape=jax.ShapeDtypeStruct((splits * splits, 1, block), jnp.float32),
        in_specs=[smem] + [vmem] * 6,
        out_specs=vmem,
        compiler_params=params,
        name="ring",
    )(index, owner_row, tile_size.reshape(1, -1), own, left, right, best)
    return jnp.max(lax.all_to_all(best, AXES, 0, 0, tiled=True, axis_index_groups=sheets), axis=0)


def solution(mesh):
    return jax.shard_map(
        local,
        mesh=mesh,
        in_specs=(P(("dp", "split"), None), P(), P(("dp", "split")), P(("dp", "split")), P(), P()),
        out_specs=P("dp", "split"),
        check_vma=False,
    )
```

```python
import jax
import jax.numpy as jnp
from jax import lax
from jax.experimental import pallas as pl
from jax.experimental.pallas import tpu as pltpu
from jax.sharding import PartitionSpec as P

TILE = 2048
EPS = 1e-06
AXES = ("dp", "split")
NT = (((1,), (1,)), ((), ()))
FAR = 1e9


def plane_order(planes):
    bits = max(planes.bit_length() - 1, 0)
    if planes != 1 << bits:
        return list(range(planes))
    return [sum((z >> i & 1) << bits - 1 - i for i in range(bits)) for z in range(planes)]


def iota(shape, dim):
    return lax.broadcasted_iota(jnp.int32, shape, dim)


def bf16(mask_or_int):
    return mask_or_int.astype(jnp.float32).astype(jnp.bfloat16)


def project_kernel(splits, block, features_hbm, weight_hbm, member_ref, owner_ref, out_ref, features, weight, semaphores):
    steps = 4
    part = features.shape[1] // steps
    spans = [slice(i * part, (i + 1) * part) for i in range(steps)]
    pairs = []
    for span in spans:
        pairs.append((weight_hbm.at[span, :], weight.at[span, :]))
        pairs.append((features_hbm.at[:, span], features.at[:, span]))
    copies = [pltpu.make_async_copy(*pair, semaphores.at[i]) for i, pair in enumerate(pairs)]
    for copy in copies:
        copy.start()
    member = member_ref[...]
    clusters, rows, width = owner_ref.shape[1], member.shape[1], weight.shape[1]
    lines = out_ref.shape[0]
    cluster, rank = member // TILE, member % TILE
    owner = bf16(jnp.broadcast_to(owner_ref[...], (8, clusters)))
    named = bf16(iota((clusters, rows), 0) == cluster)
    slot = jnp.dot(owner, named, preferred_element_type=jnp.float32)[0:1].astype(jnp.int32)
    position = jnp.zeros_like(slot)
    for i, z in enumerate(plane_order(clusters // (2 * splits))):
        position = jnp.where(slot // (2 * splits) == z, i * (2 * splits) + slot % (2 * splits), position)
    place = rank // block
    target = jnp.where(member >= 0, place % 2 * lines + position * (splits // 2) + place // 2, -1)
    chosen = bf16(iota((2 * lines, rows), 0) == target)
    high, low = (rank + 1) // 16, (rank + 1) % 16
    lane = iota((128, rows), 0)
    digits = bf16(jnp.where(lane // 2 == place % 2, jnp.where(lane % 2 == 0, high, low), 0))
    anywhere = chosen[:lines] + chosen[lines:]
    numbers = lax.dot_general(anywhere, digits, NT, preferred_element_type=jnp.float32)
    out_ref[:, 2 * width :] = numbers.astype(jnp.bfloat16)

    projected = jnp.zeros((rows, width), jnp.float32)
    for i, span in enumerate(spans):
        copies[2 * i].wait()
        copies[2 * i + 1].wait()
        projected += jnp.dot(features[:, span], weight[span, :], preferred_element_type=jnp.float32)
    normed = projected * lax.rsqrt(jnp.sum(projected * projected, axis=1, keepdims=True) + EPS)
    normed = normed.astype(jnp.bfloat16)
    sent = jnp.dot(chosen, normed, preferred_element_type=jnp.float32).astype(jnp.bfloat16)
    for i in range(2):
        out_ref[:, i * width : (i + 1) * width] = sent[i * lines : (i + 1) * lines]


class Members:
    def __init__(self, ref, width, splits):
        self.ref, self.width, self.splits, self.digits = ref, width, splits, ref[:, 2 * width :]
        self.step = ref.shape[0] // 2

    def rows(self, index):
        span = slice(index // 2 * self.step, (index // 2 + 1) * self.step)
        return self.ref[span, index % 2 * self.width : (index % 2 + 1) * self.width]

    def down(self):
        lane, digit = iota((128, 2 * self.step), 1) // self.step, iota((128, 2 * self.step), 0)
        weights = bf16(jnp.where(digit == 2 * lane, 16, jnp.where(digit == 2 * lane + 1, 1, 0)))
        found = jnp.dot(self.digits, weights, preferred_element_type=jnp.float32)
        return jnp.concatenate([found[: self.step], found[self.step :]], axis=1)

    def along(self):
        line, digit = iota((8, 128), 0), iota((8, 128), 1)
        weights = bf16(jnp.where(digit == 2 * line, 16, jnp.where(digit == 2 * line + 1, 1, 0)))
        found = lax.dot_general(weights, self.digits, NT, preferred_element_type=jnp.float32)
        return jnp.concatenate([found[0:2, : self.step], found[0:2, self.step :]], axis=0)

    def stacked(self):
        return jnp.concatenate([self.rows(a) for a in range(self.splits)], axis=0)


def earlier_max(best, members, queries):
    splits, step = len(best), queries.step
    later, numbers = queries.stacked(), queries.along()
    for part in members:
        scores = lax.dot_general(part.stacked(), later, NT, preferred_element_type=jnp.float32)
        down = part.down()
        down = jnp.where(down > 0, down, FAR)
        for b in range(splits):
            number = down[:, b * step : (b + 1) * step]
            for a in range(b, splits):
                tile = scores[b * step : (b + 1) * step, a * step : (a + 1) * step]
                found = jnp.where(number < numbers[a : a + 1], tile, -1.0)
                best[a] = jnp.maximum(best[a], jnp.max(found.reshape(-1, 8, step), axis=0))
    return best


def own_kernel(splits, width, step, own_ref, out_ref):
    own = Members(own_ref, width, splits)
    best = [jnp.full((8, step), -1.0, jnp.float32) for _ in range(splits)]
    best = earlier_max(best, [own], own)
    for a in range(splits):
        out_ref[:, a * step : (a + 1) * step] = best[a]


def side_kernel(splits, width, step, own_ref, side_ref, best_ref, out_ref):
    own, side = [Members(ref, width, splits) for ref in (own_ref, side_ref)]
    best = earlier_max([best_ref[:, a * step : (a + 1) * step] for a in range(splits)], [side], own)
    for a in range(splits):
        out_ref[:, a * step : (a + 1) * step] = best[a]


def ring_kernel(splits, width, step, index_ref, owner_ref, size_ref, own_ref, left_ref, right_ref, best_ref, out_ref):
    block = out_ref.shape[2]
    own, left, right = [Members(ref, width, splits) for ref in (own_ref, left_ref, right_ref)]
    own_best = [best_ref[:, a * step : (a + 1) * step] for a in range(splits)]
    own_best = earlier_max(own_best, [left], own)
    left_best = [jnp.full((8, step), -1.0, jnp.float32) for _ in range(splits)]
    left_best = earlier_max(left_best, [right], left)
    own_down, left_down = own.down(), left.down()

    size = jnp.sum(jnp.where(owner_ref[...] == index_ref[0], size_ref[...], 0), axis=1, keepdims=True)
    for a in range(splits):
        rank = a * block + iota((1, block), 1)
        target = (rank + 1).astype(jnp.float32)
        span = slice(a * step, (a + 1) * step)
        column = jnp.concatenate([own_down[:, span], left_down[:, span]], axis=0)
        chosen = jnp.concatenate(
            [bf16(column == target[:, i * step : (i + 1) * step]) for i in range(block // step)], axis=1
        )
        best = jnp.concatenate(
            [jnp.max(own_best[a], axis=0, keepdims=True), jnp.max(left_best[a], axis=0, keepdims=True)], axis=1
        )
        first = best.astype(jnp.bfloat16)
        rest = best - first.astype(jnp.float32)
        second = rest.astype(jnp.bfloat16)
        third = (rest - second.astype(jnp.float32)).astype(jnp.bfloat16)
        line = iota((8, best.shape[1]), 0)
        terms = jnp.ones(line.shape, jnp.float32)
        for i, term in enumerate((first, second, third)):
            terms = jnp.where(line == i, term.astype(jnp.float32), terms)
        found = jnp.dot(terms.astype(jnp.bfloat16), chosen, preferred_element_type=jnp.float32)
        ordered = found[0:1] + found[1:2] + found[2:3]
        ordered = jnp.where((found[3:4] > 0) & (rank < size), ordered, -1.0)
        for i in range(splits):
            out_ref[i * splits + a] = jnp.where(index_ref[1] == i, ordered, -1.0)


def local(features, proj_weight, row_cluster, row_rank, owner_slot, tile_size):
    owners, splits = lax.axis_size("dp"), lax.axis_size("split")
    planes = owners // (2 * splits)
    rows, width = features.shape[0], proj_weight.shape[1]
    block = TILE // splits
    hbm = pl.BlockSpec(memory_space=pltpu.HBM)
    vmem = pl.BlockSpec(memory_space=pltpu.VMEM)
    smem = pl.BlockSpec(memory_space=pltpu.SMEM)
    params = pltpu.CompilerParams(vmem_limit_bytes=32 * 1024 * 1024)
    owner_row = owner_slot.reshape(1, -1)
    member = jnp.where(row_cluster >= 0, row_cluster * TILE + row_rank, -1)

    def device(z, y, core, x):
        return ((z * splits + y) * 2 + core) * splits + x

    everywhere = [(z, a, b) for z in range(planes) for a in range(splits) for b in range(splits)]
    crosses = [
        [device(z, g, 1, j) if core else device(z, j, 0, g) for z in plane_order(planes) for j in range(splits) for core in range(2)]
        for g in range(splits)
    ]
    sheets = [
        [device(z, a, core, b) for a in range(splits) for b in range(splits)] for z in range(planes) for core in range(2)
    ]

    def shift(array, step):
        pairs = [(device(z, a, 0, b), device(z, a, 0, (b + step) % splits)) for z, a, b in everywhere]
        pairs += [(device(z, a, 1, b), device(z, (a + step) % splits, 1, b)) for z, a, b in everywhere]
        return lax.ppermute(array, AXES, pairs)

    outgoing = pl.pallas_call(
        lambda *refs: project_kernel(splits, block, *refs),
        out_shape=jax.ShapeDtypeStruct((rows // 2, 2 * width + 128), jnp.bfloat16),
        in_specs=[hbm] * 2 + [vmem] * 2,
        out_specs=vmem,
        scratch_shapes=[
            pltpu.VMEM(features.shape, jnp.bfloat16),
            pltpu.VMEM(proj_weight.shape, jnp.bfloat16),
            pltpu.SemaphoreType.DMA((8,)),
        ],
        compiler_params=pltpu.CompilerParams(vmem_limit_bytes=55200000),
        name="project",
    )(features, proj_weight, member.reshape(1, rows), owner_row)

    own = lax.all_to_all(
        outgoing.reshape(owners, splits // 2, -1), AXES, 0, 0, tiled=True, axis_index_groups=crosses
    )
    own = own.transpose(1, 0, 2).reshape(rows // 2, -1)
    left, right = shift(own, 1), shift(own, -1)

    best = pl.pallas_call(
        lambda *refs: own_kernel(splits, width, owners, *refs),
        out_shape=jax.ShapeDtypeStruct((8, splits * owners), jnp.float32),
        in_specs=[vmem],
        out_specs=vmem,
        compiler_params=params,
        name="own",
        cost_estimate=pl.CostEstimate(flops=2 * rows * rows * width, bytes_accessed=2 << 20, transcendentals=0),
    )(own)
    best = pl.pallas_call(
        lambda *refs: side_kernel(splits, width, owners, *refs),
        out_shape=jax.ShapeDtypeStruct((8, splits * owners), jnp.float32),
        in_specs=[vmem] * 3,
        out_specs=vmem,
        compiler_params=params,
        name="side",
        cost_estimate=pl.CostEstimate(flops=2 * rows * rows * width, bytes_accessed=2 << 20, transcendentals=0),
    )(own, right, best)
    owner, x = lax.axis_index("dp"), lax.axis_index("split")
    z, y, core = owner // (2 * splits), owner // 2 % splits, owner % 2
    line = jnp.where(core == 0, y, x)
    index = jnp.stack([(z * splits + line) * 2 + core, line]).astype(jnp.int32)
    best = pl.pallas_call(
        lambda *refs: ring_kernel(splits, width, owners, *refs),
        out_shape=jax.ShapeDtypeStruct((splits * splits, 1, block), jnp.float32),
        in_specs=[smem] + [vmem] * 6,
        out_specs=vmem,
        compiler_params=params,
        name="ring",
    )(index, owner_row, tile_size.reshape(1, -1), own, left, right, best)
    return jnp.max(lax.all_to_all(best, AXES, 0, 0, tiled=True, axis_index_groups=sheets), axis=0)


def solution(mesh):
    return jax.shard_map(
        local,
        mesh=mesh,
        in_specs=(P(("dp", "split"), None), P(), P(("dp", "split")), P(("dp", "split")), P(), P()),
        out_specs=P("dp", "split"),
        check_vma=False,
    )
```

```python
import jax
import jax.numpy as jnp
from jax import lax
from jax.experimental import pallas as pl
from jax.experimental.pallas import tpu as pltpu
from jax.sharding import PartitionSpec as P

TILE = 2048
EPS = 1e-06
AXES = ("dp", "split")
NT = (((1,), (1,)), ((), ()))
FAR = 1e9


def plane_order(planes):
    bits = max(planes.bit_length() - 1, 0)
    if planes != 1 << bits:
        return list(range(planes))
    return [sum((z >> i & 1) << bits - 1 - i for i in range(bits)) for z in range(planes)]


def iota(shape, dim):
    return lax.broadcasted_iota(jnp.int32, shape, dim)


def bf16(mask_or_int):
    return mask_or_int.astype(jnp.float32).astype(jnp.bfloat16)


def project_kernel(splits, block, features_hbm, weight_hbm, member_ref, owner_ref, out_ref, features, weight, semaphores):
    steps = 4
    part = features.shape[1] // steps
    spans = [slice(i * part, (i + 1) * part) for i in range(steps)]
    pairs = []
    for span in spans:
        pairs.append((weight_hbm.at[span, :], weight.at[span, :]))
        pairs.append((features_hbm.at[:, span], features.at[:, span]))
    copies = [pltpu.make_async_copy(*pair, semaphores.at[i]) for i, pair in enumerate(pairs)]
    for copy in copies:
        copy.start()
    member = member_ref[...]
    clusters, rows, width = owner_ref.shape[1], member.shape[1], weight.shape[1]
    lines = out_ref.shape[0]
    cluster, rank = member // TILE, member % TILE
    owner = bf16(jnp.broadcast_to(owner_ref[...], (8, clusters)))
    named = bf16(iota((clusters, rows), 0) == cluster)
    slot = jnp.dot(owner, named, preferred_element_type=jnp.float32)[0:1].astype(jnp.int32)
    position = jnp.zeros_like(slot)
    for i, z in enumerate(plane_order(clusters // (2 * splits))):
        position = jnp.where(slot // (2 * splits) == z, i * (2 * splits) + slot % (2 * splits), position)
    place = rank // block
    target = jnp.where(member >= 0, place % 2 * lines + position * (splits // 2) + place // 2, -1)
    chosen = bf16(iota((2 * lines, rows), 0) == target)
    high, low = (rank + 1) // 16, (rank + 1) % 16
    lane = iota((128, rows), 0)
    digits = bf16(jnp.where(lane // 2 == place % 2, jnp.where(lane % 2 == 0, high, low), 0))
    anywhere = chosen[:lines] + chosen[lines:]
    numbers = lax.dot_general(anywhere, digits, NT, preferred_element_type=jnp.float32)
    out_ref[:, 2 * width :] = numbers.astype(jnp.bfloat16)

    projected = jnp.zeros((rows, width), jnp.float32)
    for i, span in enumerate(spans):
        copies[2 * i].wait()
        copies[2 * i + 1].wait()
        projected += jnp.dot(features[:, span], weight[span, :], preferred_element_type=jnp.float32)
    normed = projected * lax.rsqrt(jnp.sum(projected * projected, axis=1, keepdims=True) + EPS)
    normed = normed.astype(jnp.bfloat16)
    sent = jnp.dot(chosen, normed, preferred_element_type=jnp.float32).astype(jnp.bfloat16)
    for i in range(2):
        out_ref[:, i * width : (i + 1) * width] = sent[i * lines : (i + 1) * lines]


class Members:
    def __init__(self, ref, width, splits):
        self.ref, self.width, self.splits, self.digits = ref, width, splits, ref[:, 2 * width :]
        self.step = ref.shape[0] // 2

    def rows(self, index):
        span = slice(index // 2 * self.step, (index // 2 + 1) * self.step)
        return self.ref[span, index % 2 * self.width : (index % 2 + 1) * self.width]

    def down(self):
        lane, digit = iota((128, 2 * self.step), 1) // self.step, iota((128, 2 * self.step), 0)
        weights = bf16(jnp.where(digit == 2 * lane, 16, jnp.where(digit == 2 * lane + 1, 1, 0)))
        found = jnp.dot(self.digits, weights, preferred_element_type=jnp.float32)
        return jnp.concatenate([found[: self.step], found[self.step :]], axis=1)

    def along(self):
        line, digit = iota((8, 128), 0), iota((8, 128), 1)
        weights = bf16(jnp.where(digit == 2 * line, 16, jnp.where(digit == 2 * line + 1, 1, 0)))
        found = lax.dot_general(weights, self.digits, NT, preferred_element_type=jnp.float32)
        return jnp.concatenate([found[0:2, : self.step], found[0:2, self.step :]], axis=0)

    def stacked(self):
        return jnp.concatenate([self.rows(a) for a in range(self.splits)], axis=0)


def earlier_max(best, members, queries):
    splits, step = len(best), queries.step
    later, numbers = queries.stacked(), queries.along()
    for part in members:
        scores = lax.dot_general(part.stacked(), later, NT, preferred_element_type=jnp.float32)
        down = part.down()
        down = jnp.where(down > 0, down, FAR)
        for b in range(splits):
            number = down[:, b * step : (b + 1) * step]
            for a in range(b, splits):
                tile = scores[b * step : (b + 1) * step, a * step : (a + 1) * step]
                found = jnp.where(number < numbers[a : a + 1], tile, -1.0)
                best[a] = jnp.maximum(best[a], jnp.max(found.reshape(-1, 8, step), axis=0))
    return best


def own_kernel(splits, width, step, own_ref, out_ref):
    own = Members(own_ref, width, splits)
    best = [jnp.full((8, step), -1.0, jnp.float32) for _ in range(splits)]
    best = earlier_max(best, [own], own)
    for a in range(splits):
        out_ref[:, a * step : (a + 1) * step] = best[a]


def side_kernel(splits, width, step, own_ref, side_ref, best_ref, out_ref):
    own, side = [Members(ref, width, splits) for ref in (own_ref, side_ref)]
    best = earlier_max([best_ref[:, a * step : (a + 1) * step] for a in range(splits)], [side], own)
    for a in range(splits):
        out_ref[:, a * step : (a + 1) * step] = best[a]


def ring_kernel(splits, width, step, index_ref, owner_ref, size_ref, own_ref, left_ref, right_ref, best_ref, out_ref):
    block = out_ref.shape[2]
    own, left, right = [Members(ref, width, splits) for ref in (own_ref, left_ref, right_ref)]
    own_best = [best_ref[:, a * step : (a + 1) * step] for a in range(splits)]
    own_best = earlier_max(own_best, [right], own)
    left_best = [jnp.full((8, step), -1.0, jnp.float32) for _ in range(splits)]
    left_best = earlier_max(left_best, [right], left)
    own_down, left_down = own.down(), left.down()

    size = jnp.sum(jnp.where(owner_ref[...] == index_ref[0], size_ref[...], 0), axis=1, keepdims=True)
    for a in range(splits):
        rank = a * block + iota((1, block), 1)
        target = (rank + 1).astype(jnp.float32)
        span = slice(a * step, (a + 1) * step)
        column = jnp.concatenate([own_down[:, span], left_down[:, span]], axis=0)
        chosen = jnp.concatenate(
            [bf16(column == target[:, i * step : (i + 1) * step]) for i in range(block // step)], axis=1
        )
        best = jnp.concatenate(
            [jnp.max(own_best[a], axis=0, keepdims=True), jnp.max(left_best[a], axis=0, keepdims=True)], axis=1
        )
        first = best.astype(jnp.bfloat16)
        rest = best - first.astype(jnp.float32)
        second = rest.astype(jnp.bfloat16)
        third = (rest - second.astype(jnp.float32)).astype(jnp.bfloat16)
        line = iota((8, best.shape[1]), 0)
        terms = jnp.ones(line.shape, jnp.float32)
        for i, term in enumerate((first, second, third)):
            terms = jnp.where(line == i, term.astype(jnp.float32), terms)
        found = jnp.dot(terms.astype(jnp.bfloat16), chosen, preferred_element_type=jnp.float32)
        ordered = found[0:1] + found[1:2] + found[2:3]
        ordered = jnp.where((found[3:4] > 0) & (rank < size), ordered, -1.0)
        for i in range(splits):
            out_ref[i * splits + a] = jnp.where(index_ref[1] == i, ordered, -1.0)


def local(features, proj_weight, row_cluster, row_rank, owner_slot, tile_size):
    owners, splits = lax.axis_size("dp"), lax.axis_size("split")
    planes = owners // (2 * splits)
    rows, width = features.shape[0], proj_weight.shape[1]
    block = TILE // splits
    hbm = pl.BlockSpec(memory_space=pltpu.HBM)
    vmem = pl.BlockSpec(memory_space=pltpu.VMEM)
    smem = pl.BlockSpec(memory_space=pltpu.SMEM)
    params = pltpu.CompilerParams(vmem_limit_bytes=32 * 1024 * 1024)
    owner_row = owner_slot.reshape(1, -1)
    member = jnp.where(row_cluster >= 0, row_cluster * TILE + row_rank, -1)

    def device(z, y, core, x):
        return ((z * splits + y) * 2 + core) * splits + x

    everywhere = [(z, a, b) for z in range(planes) for a in range(splits) for b in range(splits)]
    crosses = [
        [device(z, g, 1, j) if core else device(z, j, 0, g) for z in plane_order(planes) for j in range(splits) for core in range(2)]
        for g in range(splits)
    ]
    sheets = [
        [device(z, a, core, b) for a in range(splits) for b in range(splits)] for z in range(planes) for core in range(2)
    ]

    def shift(array, step):
        pairs = [(device(z, a, 0, b), device(z, a, 0, (b + step) % splits)) for z, a, b in everywhere]
        pairs += [(device(z, a, 1, b), device(z, (a + step) % splits, 1, b)) for z, a, b in everywhere]
        return lax.ppermute(array, AXES, pairs)

    outgoing = pl.pallas_call(
        lambda *refs: project_kernel(splits, block, *refs),
        out_shape=jax.ShapeDtypeStruct((rows // 2, 2 * width + 128), jnp.bfloat16),
        in_specs=[hbm] * 2 + [vmem] * 2,
        out_specs=vmem,
        scratch_shapes=[
            pltpu.VMEM(features.shape, jnp.bfloat16),
            pltpu.VMEM(proj_weight.shape, jnp.bfloat16),
            pltpu.SemaphoreType.DMA((8,)),
        ],
        compiler_params=pltpu.CompilerParams(vmem_limit_bytes=55200000),
        name="project",
    )(features, proj_weight, member.reshape(1, rows), owner_row)

    own = lax.all_to_all(
        outgoing.reshape(owners, splits // 2, -1), AXES, 0, 0, tiled=True, axis_index_groups=crosses
    )
    own = own.transpose(1, 0, 2).reshape(rows // 2, -1)
    left, right = shift(own, 1), shift(own, -1)

    best = pl.pallas_call(
        lambda *refs: own_kernel(splits, width, owners, *refs),
        out_shape=jax.ShapeDtypeStruct((8, splits * owners), jnp.float32),
        in_specs=[vmem],
        out_specs=vmem,
        compiler_params=params,
        name="own",
        cost_estimate=pl.CostEstimate(flops=2 * rows * rows * width, bytes_accessed=2 << 20, transcendentals=0),
    )(own)
    best = pl.pallas_call(
        lambda *refs: side_kernel(splits, width, owners, *refs),
        out_shape=jax.ShapeDtypeStruct((8, splits * owners), jnp.float32),
        in_specs=[vmem] * 3,
        out_specs=vmem,
        compiler_params=params,
        name="side",
        cost_estimate=pl.CostEstimate(flops=2 * rows * rows * width, bytes_accessed=2 << 20, transcendentals=0),
    )(own, left, best)
    owner, x = lax.axis_index("dp"), lax.axis_index("split")
    z, y, core = owner // (2 * splits), owner // 2 % splits, owner % 2
    line = jnp.where(core == 0, y, x)
    index = jnp.stack([(z * splits + line) * 2 + core, line]).astype(jnp.int32)
    best = pl.pallas_call(
        lambda *refs: ring_kernel(splits, width, owners, *refs),
        out_shape=jax.ShapeDtypeStruct((splits * splits, 1, block), jnp.float32),
        in_specs=[smem] + [vmem] * 6,
        out_specs=vmem,
        compiler_params=params,
        name="ring",
    )(index, owner_row, tile_size.reshape(1, -1), own, left, right, best)
    return jnp.max(lax.all_to_all(best, AXES, 0, 0, tiled=True, axis_index_groups=sheets), axis=0)


def solution(mesh):
    return jax.shard_map(
        local,
        mesh=mesh,
        in_specs=(P(("dp", "split"), None), P(), P(("dp", "split")), P(("dp", "split")), P(), P()),
        out_specs=P("dp", "split"),
        check_vma=False,
    )
```

```python
import jax
import jax.numpy as jnp
from jax import lax
from jax.experimental import pallas as pl
from jax.experimental.pallas import tpu as pltpu
from jax.sharding import PartitionSpec as P

TILE = 2048
EPS = 1e-06
AXES = ("dp", "split")
NT = (((1,), (1,)), ((), ()))
FAR = 1e9


def plane_order(planes):
    bits = max(planes.bit_length() - 1, 0)
    if planes != 1 << bits:
        return list(range(planes))
    return [sum((z >> i & 1) << bits - 1 - i for i in range(bits)) for z in range(planes)][::-1]


def iota(shape, dim):
    return lax.broadcasted_iota(jnp.int32, shape, dim)


def bf16(mask_or_int):
    return mask_or_int.astype(jnp.float32).astype(jnp.bfloat16)


def project_kernel(splits, block, features_hbm, weight_hbm, member_ref, owner_ref, out_ref, features, weight, semaphores):
    steps = 4
    part = features.shape[1] // steps
    spans = [slice(i * part, (i + 1) * part) for i in range(steps)]
    pairs = []
    for span in spans:
        pairs.append((weight_hbm.at[span, :], weight.at[span, :]))
        pairs.append((features_hbm.at[:, span], features.at[:, span]))
    copies = [pltpu.make_async_copy(*pair, semaphores.at[i]) for i, pair in enumerate(pairs)]
    for copy in copies:
        copy.start()
    member = member_ref[...]
    clusters, rows, width = owner_ref.shape[1], member.shape[1], weight.shape[1]
    lines = out_ref.shape[0]
    cluster, rank = member // TILE, member % TILE
    owner = bf16(jnp.broadcast_to(owner_ref[...], (8, clusters)))
    named = bf16(iota((clusters, rows), 0) == cluster)
    slot = jnp.dot(owner, named, preferred_element_type=jnp.float32)[0:1].astype(jnp.int32)
    position = jnp.zeros_like(slot)
    for i, z in enumerate(plane_order(clusters // (2 * splits))):
        position = jnp.where(slot // (2 * splits) == z, i * (2 * splits) + slot % (2 * splits), position)
    place = rank // block
    target = jnp.where(member >= 0, place % 2 * lines + position * (splits // 2) + place // 2, -1)
    chosen = bf16(iota((2 * lines, rows), 0) == target)
    high, low = (rank + 1) // 16, (rank + 1) % 16
    lane = iota((128, rows), 0)
    digits = bf16(jnp.where(lane // 2 == place % 2, jnp.where(lane % 2 == 0, high, low), 0))
    anywhere = chosen[:lines] + chosen[lines:]
    numbers = lax.dot_general(anywhere, digits, NT, preferred_element_type=jnp.float32)
    out_ref[:, 2 * width :] = numbers.astype(jnp.bfloat16)

    projected = jnp.zeros((rows, width), jnp.float32)
    for i, span in enumerate(spans):
        copies[2 * i].wait()
        copies[2 * i + 1].wait()
        projected += jnp.dot(features[:, span], weight[span, :], preferred_element_type=jnp.float32)
    normed = projected * lax.rsqrt(jnp.sum(projected * projected, axis=1, keepdims=True) + EPS)
    normed = normed.astype(jnp.bfloat16)
    sent = jnp.dot(chosen, normed, preferred_element_type=jnp.float32).astype(jnp.bfloat16)
    for i in range(2):
        out_ref[:, i * width : (i + 1) * width] = sent[i * lines : (i + 1) * lines]


class Members:
    def __init__(self, ref, width, splits):
        self.ref, self.width, self.splits, self.digits = ref, width, splits, ref[:, 2 * width :]
        self.step = ref.shape[0] // 2

    def rows(self, index):
        span = slice(index // 2 * self.step, (index // 2 + 1) * self.step)
        return self.ref[span, index % 2 * self.width : (index % 2 + 1) * self.width]

    def down(self):
        lane, digit = iota((128, 2 * self.step), 1) // self.step, iota((128, 2 * self.step), 0)
        weights = bf16(jnp.where(digit == 2 * lane, 16, jnp.where(digit == 2 * lane + 1, 1, 0)))
        found = jnp.dot(self.digits, weights, preferred_element_type=jnp.float32)
        return jnp.concatenate([found[: self.step], found[self.step :]], axis=1)

    def along(self):
        line, digit = iota((8, 128), 0), iota((8, 128), 1)
        weights = bf16(jnp.where(digit == 2 * line, 16, jnp.where(digit == 2 * line + 1, 1, 0)))
        found = lax.dot_general(weights, self.digits, NT, preferred_element_type=jnp.float32)
        return jnp.concatenate([found[0:2, : self.step], found[0:2, self.step :]], axis=0)

    def stacked(self):
        return jnp.concatenate([self.rows(a) for a in range(self.splits)], axis=0)


def earlier_max(best, members, queries):
    splits, step = len(best), queries.step
    later, numbers = queries.stacked(), queries.along()
    for part in members:
        scores = lax.dot_general(part.stacked(), later, NT, preferred_element_type=jnp.float32)
        down = part.down()
        down = jnp.where(down > 0, down, FAR)
        for b in range(splits):
            number = down[:, b * step : (b + 1) * step]
            for a in range(b, splits):
                tile = scores[b * step : (b + 1) * step, a * step : (a + 1) * step]
                found = jnp.where(number < numbers[a : a + 1], tile, -1.0)
                best[a] = jnp.maximum(best[a], jnp.max(found.reshape(-1, 8, step), axis=0))
    return best


def own_kernel(splits, width, step, own_ref, out_ref):
    own = Members(own_ref, width, splits)
    best = [jnp.full((8, step), -1.0, jnp.float32) for _ in range(splits)]
    best = earlier_max(best, [own], own)
    for a in range(splits):
        out_ref[:, a * step : (a + 1) * step] = best[a]


def side_kernel(splits, width, step, own_ref, side_ref, best_ref, out_ref):
    own, side = [Members(ref, width, splits) for ref in (own_ref, side_ref)]
    best = earlier_max([best_ref[:, a * step : (a + 1) * step] for a in range(splits)], [side], own)
    for a in range(splits):
        out_ref[:, a * step : (a + 1) * step] = best[a]


def ring_kernel(splits, width, step, index_ref, owner_ref, size_ref, own_ref, left_ref, right_ref, best_ref, out_ref):
    block = out_ref.shape[2]
    own, left, right = [Members(ref, width, splits) for ref in (own_ref, left_ref, right_ref)]
    own_best = [best_ref[:, a * step : (a + 1) * step] for a in range(splits)]
    own_best = earlier_max(own_best, [right], own)
    left_best = [jnp.full((8, step), -1.0, jnp.float32) for _ in range(splits)]
    left_best = earlier_max(left_best, [right], left)
    own_down, left_down = own.down(), left.down()

    size = jnp.sum(jnp.where(owner_ref[...] == index_ref[0], size_ref[...], 0), axis=1, keepdims=True)
    for a in range(splits):
        rank = a * block + iota((1, block), 1)
        target = (rank + 1).astype(jnp.float32)
        span = slice(a * step, (a + 1) * step)
        column = jnp.concatenate([own_down[:, span], left_down[:, span]], axis=0)
        chosen = jnp.concatenate(
            [bf16(column == target[:, i * step : (i + 1) * step]) for i in range(block // step)], axis=1
        )
        best = jnp.concatenate(
            [jnp.max(own_best[a], axis=0, keepdims=True), jnp.max(left_best[a], axis=0, keepdims=True)], axis=1
        )
        first = best.astype(jnp.bfloat16)
        rest = best - first.astype(jnp.float32)
        second = rest.astype(jnp.bfloat16)
        third = (rest - second.astype(jnp.float32)).astype(jnp.bfloat16)
        line = iota((8, best.shape[1]), 0)
        terms = jnp.ones(line.shape, jnp.float32)
        for i, term in enumerate((first, second, third)):
            terms = jnp.where(line == i, term.astype(jnp.float32), terms)
        found = jnp.dot(terms.astype(jnp.bfloat16), chosen, preferred_element_type=jnp.float32)
        ordered = found[0:1] + found[1:2] + found[2:3]
        ordered = jnp.where((found[3:4] > 0) & (rank < size), ordered, -1.0)
        for i in range(splits):
            out_ref[i * splits + a] = jnp.where(index_ref[1] == i, ordered, -1.0)


def local(features, proj_weight, row_cluster, row_rank, owner_slot, tile_size):
    owners, splits = lax.axis_size("dp"), lax.axis_size("split")
    planes = owners // (2 * splits)
    rows, width = features.shape[0], proj_weight.shape[1]
    block = TILE // splits
    hbm = pl.BlockSpec(memory_space=pltpu.HBM)
    vmem = pl.BlockSpec(memory_space=pltpu.VMEM)
    smem = pl.BlockSpec(memory_space=pltpu.SMEM)
    params = pltpu.CompilerParams(vmem_limit_bytes=32 * 1024 * 1024)
    owner_row = owner_slot.reshape(1, -1)
    member = jnp.where(row_cluster >= 0, row_cluster * TILE + row_rank, -1)

    def device(z, y, core, x):
        return ((z * splits + y) * 2 + core) * splits + x

    everywhere = [(z, a, b) for z in range(planes) for a in range(splits) for b in range(splits)]
    crosses = [
        [device(z, g, 1, j) if core else device(z, j, 0, g) for z in plane_order(planes) for j in range(splits) for core in range(2)]
        for g in range(splits)
    ]
    sheets = [
        [device(z, a, core, b) for a in range(splits) for b in range(splits)] for z in range(planes) for core in range(2)
    ]

    def shift(array, step):
        pairs = [(device(z, a, 0, b), device(z, a, 0, (b + step) % splits)) for z, a, b in everywhere]
        pairs += [(device(z, a, 1, b), device(z, (a + step) % splits, 1, b)) for z, a, b in everywhere]
        return lax.ppermute(array, AXES, pairs)

    outgoing = pl.pallas_call(
        lambda *refs: project_kernel(splits, block, *refs),
        out_shape=jax.ShapeDtypeStruct((rows // 2, 2 * width + 128), jnp.bfloat16),
        in_specs=[hbm] * 2 + [vmem] * 2,
        out_specs=vmem,
        scratch_shapes=[
            pltpu.VMEM(features.shape, jnp.bfloat16),
            pltpu.VMEM(proj_weight.shape, jnp.bfloat16),
            pltpu.SemaphoreType.DMA((8,)),
        ],
        compiler_params=pltpu.CompilerParams(vmem_limit_bytes=55200000),
        name="project",
    )(features, proj_weight, member.reshape(1, rows), owner_row)

    own = lax.all_to_all(
        outgoing.reshape(owners, splits // 2, -1), AXES, 0, 0, tiled=True, axis_index_groups=crosses
    )
    own = own.transpose(1, 0, 2).reshape(rows // 2, -1)
    left, right = shift(own, 1), shift(own, -1)

    best = pl.pallas_call(
        lambda *refs: own_kernel(splits, width, owners, *refs),
        out_shape=jax.ShapeDtypeStruct((8, splits * owners), jnp.float32),
        in_specs=[vmem],
        out_specs=vmem,
        compiler_params=params,
        name="own",
        cost_estimate=pl.CostEstimate(flops=2 * rows * rows * width, bytes_accessed=2 << 20, transcendentals=0),
    )(own)
    best = pl.pallas_call(
        lambda *refs: side_kernel(splits, width, owners, *refs),
        out_shape=jax.ShapeDtypeStruct((8, splits * owners), jnp.float32),
        in_specs=[vmem] * 3,
        out_specs=vmem,
        compiler_params=params,
        name="side",
        cost_estimate=pl.CostEstimate(flops=2 * rows * rows * width, bytes_accessed=2 << 20, transcendentals=0),
    )(own, left, best)
    owner, x = lax.axis_index("dp"), lax.axis_index("split")
    z, y, core = owner // (2 * splits), owner // 2 % splits, owner % 2
    line = jnp.where(core == 0, y, x)
    index = jnp.stack([(z * splits + line) * 2 + core, line]).astype(jnp.int32)
    best = pl.pallas_call(
        lambda *refs: ring_kernel(splits, width, owners, *refs),
        out_shape=jax.ShapeDtypeStruct((splits * splits, 1, block), jnp.float32),
        in_specs=[smem] + [vmem] * 6,
        out_specs=vmem,
        compiler_params=params,
        name="ring",
    )(index, owner_row, tile_size.reshape(1, -1), own, left, right, best)
    return jnp.max(lax.all_to_all(best, AXES, 0, 0, tiled=True, axis_index_groups=sheets), axis=0)


def solution(mesh):
    return jax.shard_map(
        local,
        mesh=mesh,
        in_specs=(P(("dp", "split"), None), P(), P(("dp", "split")), P(("dp", "split")), P(), P()),
        out_specs=P("dp", "split"),
        check_vma=False,
    )
```

```python
import jax
import jax.numpy as jnp
from jax import lax
from jax.experimental import pallas as pl
from jax.experimental.pallas import tpu as pltpu
from jax.sharding import PartitionSpec as P

TILE = 2048
EPS = 1e-06
AXES = ("dp", "split")
NT = (((1,), (1,)), ((), ()))
FAR = 1e9


def plane_order(planes):
    bits = max(planes.bit_length() - 1, 0)
    if planes != 1 << bits:
        return list(range(planes))
    return [sum((z >> i & 1) << bits - 1 - i for i in range(bits)) for z in range(planes)][::-1]


def iota(shape, dim):
    return lax.broadcasted_iota(jnp.int32, shape, dim)


def bf16(mask_or_int):
    return mask_or_int.astype(jnp.float32).astype(jnp.bfloat16)


def project_kernel(splits, block, features_hbm, weight_hbm, member_ref, owner_ref, out_ref, features, weight, semaphores):
    steps = 4
    part = features.shape[1] // steps
    spans = [slice(i * part, (i + 1) * part) for i in range(steps)]
    pairs = []
    for span in spans:
        pairs.append((weight_hbm.at[span, :], weight.at[span, :]))
        pairs.append((features_hbm.at[:, span], features.at[:, span]))
    copies = [pltpu.make_async_copy(*pair, semaphores.at[i]) for i, pair in enumerate(pairs)]
    for copy in copies:
        copy.start()
    member = member_ref[...]
    clusters, rows, width = owner_ref.shape[1], member.shape[1], weight.shape[1]
    lines = out_ref.shape[0]
    cluster, rank = member // TILE, member % TILE
    owner = bf16(jnp.broadcast_to(owner_ref[...], (8, clusters)))
    named = bf16(iota((clusters, rows), 0) == cluster)
    slot = jnp.dot(owner, named, preferred_element_type=jnp.float32)[0:1].astype(jnp.int32)
    position = jnp.zeros_like(slot)
    for i, z in enumerate(plane_order(clusters // (2 * splits))):
        position = jnp.where(slot // (2 * splits) == z, i * (2 * splits) + slot % (2 * splits), position)
    place = rank // block
    target = jnp.where(member >= 0, place % 2 * lines + position * (splits // 2) + place // 2, -1)
    chosen = bf16(iota((2 * lines, rows), 0) == target)
    high, low = (rank + 1) // 16, (rank + 1) % 16
    lane = iota((128, rows), 0)
    digits = bf16(jnp.where(lane // 2 == place % 2, jnp.where(lane % 2 == 0, high, low), 0))
    anywhere = chosen[:lines] + chosen[lines:]
    numbers = lax.dot_general(anywhere, digits, NT, preferred_element_type=jnp.float32)
    out_ref[:, 2 * width :] = numbers.astype(jnp.bfloat16)

    projected = jnp.zeros((rows, width), jnp.float32)
    for i, span in enumerate(spans):
        copies[2 * i].wait()
        copies[2 * i + 1].wait()
        projected += jnp.dot(features[:, span], weight[span, :], preferred_element_type=jnp.float32)
    normed = projected * lax.rsqrt(jnp.sum(projected * projected, axis=1, keepdims=True) + EPS)
    normed = normed.astype(jnp.bfloat16)
    sent = jnp.dot(chosen, normed, preferred_element_type=jnp.float32).astype(jnp.bfloat16)
    for i in range(2):
        out_ref[:, i * width : (i + 1) * width] = sent[i * lines : (i + 1) * lines]


class Members:
    def __init__(self, ref, width, splits):
        self.ref, self.width, self.splits, self.digits = ref, width, splits, ref[:, 2 * width :]
        self.step = ref.shape[0] // 2

    def rows(self, index):
        span = slice(index // 2 * self.step, (index // 2 + 1) * self.step)
        return self.ref[span, index % 2 * self.width : (index % 2 + 1) * self.width]

    def down(self):
        lane, digit = iota((128, 2 * self.step), 1) // self.step, iota((128, 2 * self.step), 0)
        weights = bf16(jnp.where(digit == 2 * lane, 16, jnp.where(digit == 2 * lane + 1, 1, 0)))
        found = jnp.dot(self.digits, weights, preferred_element_type=jnp.float32)
        return jnp.concatenate([found[: self.step], found[self.step :]], axis=1)

    def along(self):
        line, digit = iota((8, 128), 0), iota((8, 128), 1)
        weights = bf16(jnp.where(digit == 2 * line, 16, jnp.where(digit == 2 * line + 1, 1, 0)))
        found = lax.dot_general(weights, self.digits, NT, preferred_element_type=jnp.float32)
        return jnp.concatenate([found[0:2, : self.step], found[0:2, self.step :]], axis=0)

    def stacked(self):
        return jnp.concatenate([self.rows(a) for a in range(self.splits)], axis=0)


def earlier_max(best, members, queries):
    splits, step = len(best), queries.step
    later, numbers = queries.stacked(), queries.along()
    for part in members:
        scores = lax.dot_general(part.stacked(), later, NT, preferred_element_type=jnp.float32)
        down = part.down()
        down = jnp.where(down > 0, down, FAR)
        for b in range(splits):
            number = down[:, b * step : (b + 1) * step]
            for a in range(b, splits):
                tile = scores[b * step : (b + 1) * step, a * step : (a + 1) * step]
                found = jnp.where(number < numbers[a : a + 1], tile, -1.0)
                best[a] = jnp.maximum(best[a], jnp.max(found.reshape(-1, 8, step), axis=0))
    return best


def own_kernel(splits, width, step, own_ref, out_ref):
    own = Members(own_ref, width, splits)
    best = [jnp.full((8, step), -1.0, jnp.float32) for _ in range(splits)]
    best = earlier_max(best, [own], own)
    for a in range(splits):
        out_ref[:, a * step : (a + 1) * step] = best[a]


def side_kernel(splits, width, step, own_ref, side_ref, best_ref, out_ref):
    own, side = [Members(ref, width, splits) for ref in (own_ref, side_ref)]
    best = earlier_max([best_ref[:, a * step : (a + 1) * step] for a in range(splits)], [side], own)
    for a in range(splits):
        out_ref[:, a * step : (a + 1) * step] = best[a]


def ring_kernel(splits, width, step, index_ref, owner_ref, size_ref, own_ref, left_ref, right_ref, best_ref, out_ref):
    block = out_ref.shape[2]
    own, left, right = [Members(ref, width, splits) for ref in (own_ref, left_ref, right_ref)]
    own_best = [best_ref[:, a * step : (a + 1) * step] for a in range(splits)]
    own_best = earlier_max(own_best, [right], own)
    left_best = [jnp.full((8, step), -1.0, jnp.float32) for _ in range(splits)]
    left_best = earlier_max(left_best, [right], left)
    own_down, left_down = own.down(), left.down()

    size = jnp.sum(jnp.where(owner_ref[...] == index_ref[0], size_ref[...], 0), axis=1, keepdims=True)
    for a in range(splits):
        rank = a * block + iota((1, block), 1)
        target = (rank + 1).astype(jnp.float32)
        span = slice(a * step, (a + 1) * step)
        column = jnp.concatenate([own_down[:, span], left_down[:, span]], axis=0)
        chosen = jnp.concatenate(
            [bf16(column == target[:, i * step : (i + 1) * step]) for i in range(block // step)], axis=1
        )
        best = jnp.concatenate(
            [jnp.max(own_best[a], axis=0, keepdims=True), jnp.max(left_best[a], axis=0, keepdims=True)], axis=1
        )
        first = best.astype(jnp.bfloat16)
        rest = best - first.astype(jnp.float32)
        second = rest.astype(jnp.bfloat16)
        third = (rest - second.astype(jnp.float32)).astype(jnp.bfloat16)
        line = iota((8, best.shape[1]), 0)
        terms = jnp.ones(line.shape, jnp.float32)
        for i, term in enumerate((first, second, third)):
            terms = jnp.where(line == i, term.astype(jnp.float32), terms)
        found = jnp.dot(terms.astype(jnp.bfloat16), chosen, preferred_element_type=jnp.float32)
        ordered = found[0:1] + found[1:2] + found[2:3]
        ordered = jnp.where((found[3:4] > 0) & (rank < size), ordered, -1.0)
        for i in range(splits):
            out_ref[splits * splits - 1 - (i * splits + a)] = jnp.where(index_ref[1] == i, ordered, -1.0)


def local(features, proj_weight, row_cluster, row_rank, owner_slot, tile_size):
    owners, splits = lax.axis_size("dp"), lax.axis_size("split")
    planes = owners // (2 * splits)
    rows, width = features.shape[0], proj_weight.shape[1]
    block = TILE // splits
    hbm = pl.BlockSpec(memory_space=pltpu.HBM)
    vmem = pl.BlockSpec(memory_space=pltpu.VMEM)
    smem = pl.BlockSpec(memory_space=pltpu.SMEM)
    params = pltpu.CompilerParams(vmem_limit_bytes=32 * 1024 * 1024)
    owner_row = owner_slot.reshape(1, -1)
    member = jnp.where(row_cluster >= 0, row_cluster * TILE + row_rank, -1)

    def device(z, y, core, x):
        return ((z * splits + y) * 2 + core) * splits + x

    everywhere = [(z, a, b) for z in range(planes) for a in range(splits) for b in range(splits)]
    crosses = [
        [device(z, g, 1, j) if core else device(z, j, 0, g) for z in plane_order(planes) for j in range(splits) for core in range(2)]
        for g in range(splits)
    ]
    sheets = [
        [device(z, a, core, b) for a in range(splits) for b in range(splits)][::-1] for z in range(planes) for core in range(2)
    ]

    def shift(array, step):
        pairs = [(device(z, a, 0, b), device(z, a, 0, (b + step) % splits)) for z, a, b in everywhere]
        pairs += [(device(z, a, 1, b), device(z, (a + step) % splits, 1, b)) for z, a, b in everywhere]
        return lax.ppermute(array, AXES, pairs)

    outgoing = pl.pallas_call(
        lambda *refs: project_kernel(splits, block, *refs),
        out_shape=jax.ShapeDtypeStruct((rows // 2, 2 * width + 128), jnp.bfloat16),
        in_specs=[hbm] * 2 + [vmem] * 2,
        out_specs=vmem,
        scratch_shapes=[
            pltpu.VMEM(features.shape, jnp.bfloat16),
            pltpu.VMEM(proj_weight.shape, jnp.bfloat16),
            pltpu.SemaphoreType.DMA((8,)),
        ],
        compiler_params=pltpu.CompilerParams(vmem_limit_bytes=55200000),
        name="project",
    )(features, proj_weight, member.reshape(1, rows), owner_row)

    own = lax.all_to_all(
        outgoing.reshape(owners, splits // 2, -1), AXES, 0, 0, tiled=True, axis_index_groups=crosses
    )
    own = own.transpose(1, 0, 2).reshape(rows // 2, -1)
    left, right = shift(own, 1), shift(own, -1)

    best = pl.pallas_call(
        lambda *refs: own_kernel(splits, width, owners, *refs),
        out_shape=jax.ShapeDtypeStruct((8, splits * owners), jnp.float32),
        in_specs=[vmem],
        out_specs=vmem,
        compiler_params=params,
        name="own",
        cost_estimate=pl.CostEstimate(flops=2 * rows * rows * width, bytes_accessed=2 << 20, transcendentals=0),
    )(own)
    best = pl.pallas_call(
        lambda *refs: side_kernel(splits, width, owners, *refs),
        out_shape=jax.ShapeDtypeStruct((8, splits * owners), jnp.float32),
        in_specs=[vmem] * 3,
        out_specs=vmem,
        compiler_params=params,
        name="side",
        cost_estimate=pl.CostEstimate(flops=2 * rows * rows * width, bytes_accessed=2 << 20, transcendentals=0),
    )(own, left, best)
    owner, x = lax.axis_index("dp"), lax.axis_index("split")
    z, y, core = owner // (2 * splits), owner // 2 % splits, owner % 2
    line = jnp.where(core == 0, y, x)
    index = jnp.stack([(z * splits + line) * 2 + core, line]).astype(jnp.int32)
    best = pl.pallas_call(
        lambda *refs: ring_kernel(splits, width, owners, *refs),
        out_shape=jax.ShapeDtypeStruct((splits * splits, 1, block), jnp.float32),
        in_specs=[smem] + [vmem] * 6,
        out_specs=vmem,
        compiler_params=params,
        name="ring",
    )(index, owner_row, tile_size.reshape(1, -1), own, left, right, best)
    return jnp.max(lax.all_to_all(best, AXES, 0, 0, tiled=True, axis_index_groups=sheets), axis=0)


def solution(mesh):
    return jax.shard_map(
        local,
        mesh=mesh,
        in_specs=(P(("dp", "split"), None), P(), P(("dp", "split")), P(("dp", "split")), P(), P()),
        out_specs=P("dp", "split"),
        check_vma=False,
    )
```
